256 devices in a mesh: section: 8 (over z_hi, x), dp: 32 (over z_lo, y, core).
Axes of the slice: x: 4, y: 4, z: 8 (z_hi: 2, z_lo: 4; z = z_hi * 4 + z_lo), core: 2. Of those that a mesh axis runs over, the one named last changes fastest.
Arguments:
- hidden: bfloat16 [8, 8192, 8192], P('section', 'dp'), may hold values from -64 to 64
- norm_gain: bfloat16 [8, 8192], P('section', 'dp'), may hold values from 0.099609375 to 1.8984375
- key_weight: bfloat16 [8, 8192, 512], P('section', 'dp'), may hold values from -0.0625 to 0.0625
- key_cotangent: bfloat16 [8, 8192, 512], P('section', 'dp'), may hold values from -24 to 24
- token_logratio: float32 [8, 8192], P('section', 'dp'), may hold values from -4 to 4
- lengths: int32 [8, 4], P('section'), may hold values from 512 to 2048
- pair_of_row: int32 [8, 4], P('section'), may hold values from 0 to 1, as said below
Outputs:
- upstream_cotangent: bfloat16 [8, 8192, 8192], P('section', 'dp')
- key_weight_grad: bfloat16 [8, 8192, 512], P('section', 'dp')
- gain_grad: bfloat16 [8, 8192], P('section', 'dp')
The draws below stay inside these ranges and needn't reach their ends.
Inputs may be any that keep to these rules, and one draw needn't show every extreme that they name: `pair_of_row`: in each section every pair number appears once among the first 2 rows and once among the last 2 rows.
All inputs are finite; a program needn't handle non-finite values.
Results may differ from the reference program's by a relative error of at most 0.029.
Values may be sent and summed in bfloat16 or wider, within the bound.
No kernel may reach another device: no remote copies, remote signals or barrier semaphores. Data moves between devices by JAX's collectives and lax.ppermute only.
A program may use at most 128 MiB of HBM per device.

```python
import math
import jax
import jax.numpy as jnp
from jax import lax

D = 8192
ROW_LEN = 2048
TOK_DEV = 256
KW = 512
SECTIONS = 8
TOKENS = 8192
ROWS = 4
PAIRS = 2


def draw_hidden(key, part):
    key = jax.random.fold_in(key, 11)
    first, second, third = jax.random.split(key, 3)
    col_scale = jnp.exp(jax.random.uniform(second, (SECTIONS, 1, D), jnp.float32, math.log(0.3), math.log(3.0)))
    row_scale = jnp.exp(jax.random.uniform(first, (SECTIONS, TOKENS, 1), jnp.float32, math.log(0.3), math.log(3.0)))
    base = jnp.clip(jax.random.normal(third, (SECTIONS, TOKENS, D), jnp.float32), -6.0, 6.0)
    values = base * row_scale * col_scale
    return values.astype(jnp.bfloat16)


def draw_token_logratio(key, part):
    key = jax.random.fold_in(key, 23)
    noise_key, offset_key = jax.random.split(key)
    places = jnp.arange(TOKENS, dtype=jnp.int32)
    offsets = (places % ROW_LEN).astype(jnp.float32)
    row_ids = places // ROW_LEN
    scale = 0.2 * jnp.exp(math.log(3.0) * offsets / ROW_LEN)
    row_offset = jax.random.uniform(offset_key, (SECTIONS, ROWS), jnp.float32, -1.0, 1.0) * (24.0 / ROW_LEN)
    row_hot = (row_ids[:, None] == jnp.arange(ROWS, dtype=jnp.int32)[None, :]).astype(jnp.float32)
    token_offset = jnp.sum(row_offset[:, None, :] * row_hot[None, :, :], axis=2)
    base = jnp.clip(jax.random.normal(noise_key, (SECTIONS, TOKENS), jnp.float32), -5.0, 5.0)
    values = base * scale[None, :]
    values = jnp.clip(values + token_offset, -4.0, 4.0)
    return values.astype(jnp.float32)


def draw_pair_of_row(key, part):
    key = jax.random.fold_in(key, 37)
    section_keys = jax.random.split(key, SECTIONS)

    def one_section(section_key):
        chosen_key, rejected_key = jax.random.split(section_key)
        chosen = jax.random.permutation(chosen_key, PAIRS)
        rejected = jax.random.permutation(rejected_key, PAIRS)
        return jnp.concatenate([chosen, rejected]).astype(jnp.int32)
    return jax.vmap(one_section)(section_keys)


def set_ends(values, key, least, high):
    longest = values.shape.index(max(values.shape))
    spots = []
    for shift in (0, 1):
        where = [jax.random.randint(jax.random.fold_in(key, axis), (), 0, length) for axis, length in enumerate(values.shape)]
        where[longest] = (where[longest] + shift) % values.shape[longest]
        spots.append(tuple(where))
    return values.at[spots[0]].set(least).at[spots[1]].set(high)


def level_of(own_key, shape, shards, least, largest):
    def one(position, blocks):
        steps = jax.random.uniform(jax.random.fold_in(jax.random.fold_in(own_key, 6), position), (blocks,), jnp.float32, least / len(shards), largest / len(shards))
        return jnp.repeat(jnp.exp(steps), shape[position] // blocks).reshape((-1,) + (1,) * (len(shape) - position - 1))

    gain = one(*shards[0])
    for cut in shards[1:]:
        gain = gain * one(*cut)
    return gain


def normal_values(rng, shape, spread, most, shards=(), kind=jnp.bfloat16):
    drawn = jax.random.normal(rng, shape, jnp.float32) * spread
    if len(shards) > 0:
        drawn = level_of(rng, shape, shards, -0.22, 0.18) * drawn
    return jnp.clip(drawn, min=-most, max=most).astype(kind)


def setup_inputs(seed: int = 0) -> dict:
    streams_of = jax.random.split(jax.random.key(seed), 8)
    return {
        "hidden": draw_hidden(jax.random.fold_in(streams_of[7], 71), 0),
        "norm_gain": jnp.clip(1.0 + 0.18 * jax.random.normal(streams_of[1], (SECTIONS, D), jnp.float32), 0.099609375, 1.8984375).astype(jnp.bfloat16),
        "key_weight": normal_values(streams_of[2], (SECTIONS, D, KW), D ** -0.5, 0.0625, ((0, 8), (1, 32))),
        "key_cotangent": normal_values(streams_of[3], (SECTIONS, TOKENS, KW), 4.0, 24.0, ((0, 8), (1, 32))),
        "token_logratio": draw_token_logratio(jax.random.fold_in(streams_of[7], 71), 0),
        "lengths": set_ends(jax.random.randint(streams_of[5], (SECTIONS, ROWS), ROW_LEN // 4, ROW_LEN + 1), jax.random.fold_in(streams_of[5], 1), ROW_LEN // 4, ROW_LEN).astype(jnp.int32),
        "pair_of_row": draw_pair_of_row(jax.random.fold_in(streams_of[7], 71), 0),
    }


DPO_BETA = 0.1

def pair_coefficients(row_ratio, pairing, pair_count):
    row_total = row_ratio.shape[0]
    signs = jnp.where(jnp.arange(row_total) < pair_count, 1.0, -1.0).astype(jnp.float32)
    pair_hot = (pairing[:, None] == jnp.arange(pair_count, dtype=jnp.int32)[None, :]).astype(jnp.float32)
    margin = lax.optimization_barrier(jnp.sum(pair_hot * (signs * row_ratio)[:, None], axis=0))
    row_margin = lax.optimization_barrier(jnp.sum(pair_hot * margin[None, :], axis=1))
    return -DPO_BETA * signs * jax.nn.sigmoid(-DPO_BETA * row_margin)

def section_pass(states, gains, weights, key_in, ratios, limits, pairing):
    token_total = states.shape[0]
    row_total = limits.shape[0]
    places = jnp.arange(token_total, dtype=jnp.int32)
    row_ids = places // ROW_LEN
    offsets = places % ROW_LEN
    member = row_ids[:, None] == jnp.arange(row_total, dtype=jnp.int32)[None, :]
    limit_tok = lax.optimization_barrier(jnp.sum(jnp.where(member, limits[None, :], 0), axis=1))
    valid = (offsets < limit_tok).astype(jnp.float32)
    row_ratio = lax.optimization_barrier(jnp.sum(jnp.where(member, (valid * ratios)[:, None], 0.0), axis=0))
    coef_rows = pair_coefficients(row_ratio, pairing, row_total // 2)
    token_weight = valid * lax.optimization_barrier(jnp.sum(jnp.where(member, coef_rows[None, :], 0.0), axis=1))
    hidden32 = states.astype(jnp.float32)
    inv_rms = lax.rsqrt(lax.optimization_barrier(jnp.mean(hidden32 * hidden32, axis=1, keepdims=True)) + 1e-06)
    unit = hidden32 * inv_rms
    gain32 = gains.astype(jnp.float32)
    normed = (unit * gain32[None, :]).astype(jnp.bfloat16)
    key_grad = (key_in.astype(jnp.float32) * token_weight[:, None]).astype(jnp.bfloat16)
    normed_grad = jnp.dot(key_grad, weights.T, preferred_element_type=jnp.float32).astype(jnp.bfloat16)
    blocks = token_total // TOK_DEV
    normed_blocks = normed.reshape(blocks, TOK_DEV, normed.shape[1])
    key_blocks = key_grad.reshape(blocks, TOK_DEV, key_grad.shape[1])
    grad_blocks = normed_grad.reshape(blocks, TOK_DEV, normed.shape[1])
    unit_blocks = unit.reshape(blocks, TOK_DEV, normed.shape[1])

    def add_block(totals, pieces):
        normed_blk, key_blk, grad_blk, unit_blk = pieces
        weight_term = jnp.dot(normed_blk.T, key_blk, preferred_element_type=jnp.float32).astype(jnp.bfloat16)
        gain_term = lax.optimization_barrier(jnp.sum(grad_blk.astype(jnp.float32) * unit_blk, axis=0)).astype(jnp.bfloat16)
        weight_term, gain_term = lax.optimization_barrier((weight_term, gain_term))
        return ((totals[0] + weight_term.astype(jnp.float32), totals[1] + gain_term.astype(jnp.float32)), None)
    start_totals = (jnp.zeros((normed.shape[1], key_grad.shape[1]), jnp.float32), jnp.zeros((normed.shape[1],), jnp.float32))
    (weight_grad, gain_grad), _ = lax.scan(add_block, start_totals, (normed_blocks, key_blocks, grad_blocks, unit_blocks))
    unit_grad = normed_grad.astype(jnp.float32) * gain32[None, :]
    inner = lax.optimization_barrier(jnp.mean(unit_grad * unit, axis=1, keepdims=True))
    section_grad = (inv_rms * (unit_grad - unit * inner)).astype(jnp.bfloat16)
    return (section_grad, weight_grad.astype(jnp.bfloat16), gain_grad.astype(jnp.bfloat16))

def reference(hidden, norm_gain, key_weight, key_cotangent, token_logratio, lengths, pair_of_row):
    section_grads = []
    weight_grads = []
    gain_grads = []
    for section_id in range(SECTIONS):
        section_grad, weight_grad, gain_grad = section_pass(hidden[section_id], norm_gain[section_id], key_weight[section_id], key_cotangent[section_id], token_logratio[section_id], lengths[section_id], pair_of_row[section_id])
        section_grads.append(section_grad)
        weight_grads.append(weight_grad)
        gain_grads.append(gain_grad)
    shifted = section_grads[1:] + [jnp.zeros_like(section_grads[0])]
    return (jnp.stack(shifted), jnp.stack(weight_grads), jnp.stack(gain_grads))
```

```python
import functools
import jax
import jax.numpy as jnp
from jax import lax
from jax.experimental import pallas as pl
from jax.experimental.pallas import tpu as pltpu
from jax.sharding import PartitionSpec as P

ROW_LEN = 2048
DPO_BETA = 0.1
EPS = 1e-06
AXES = ("section", "dp")
BF, F32 = jnp.bfloat16, jnp.float32
BLK = 256
PIECE = 16
FREE = pl.CostEstimate(flops=0, bytes_accessed=0, transcendentals=0)
EXTRA = 16
OWN = 16
VMEM_LIMIT = 56 * 1024 * 1024


def index_of(z_hi, x, z_lo, y, core):
    return ((z_hi * 4 + x) * 4 + z_lo) * 8 + y * 2 + core


def moved(value, target):
    pairs = []
    for z_hi in range(2):
        for x in range(4):
            for z_lo in range(4):
                for y in range(4):
                    for core in range(2):
                        goal = target(z_hi, x, z_lo, y, core)
                        if goal is not None:
                            pairs.append((index_of(z_hi, x, z_lo, y, core), index_of(*goal)))
    return lax.ppermute(value, AXES, pairs)


def to_previous(value):
    def target(z_hi, x, z_lo, y, core):
        section = z_hi * 4 + x - 1
        return None if section < 0 else (section // 4, section % 4, z_lo, y, core)

    return moved(value, target)


ANYWHERE = pl.BlockSpec(memory_space=pl.ANY)


def gated(values, events):
    count = len(values)
    return pl.pallas_call(
        lambda *refs: None,
        in_specs=[ANYWHERE] * (count + len(events)),
        out_specs=[ANYWHERE] * count,
        out_shape=[jax.ShapeDtypeStruct(v.shape, v.dtype) for v in values],
        input_output_aliases={i: i for i in range(count)},
        cost_estimate=FREE,
    )(*values, *events)


def stepped(value, source, goal):
    return moved(
        value,
        lambda z_hi, x, z_lo, y, core: (*goal, z_lo, y, core) if (z_hi, x) == source else None,
    )


def lowered_part(value, event):
    return moved(
        gated([value], [event])[0],
        lambda z_hi, x, z_lo, y, core: (z_hi, x - 1, z_lo, y, core) if x else None,
    )


def prepare_kernel(place, limits, pairs, weights, gains, keys, ratios, out, mark):
    tokens, kw = keys.shape
    out[:tokens, :] = (weights[...].astype(F32) * gains[...].astype(F32)).astype(BF)
    limit = limits[place[2]] - place[3]
    valid = lax.broadcasted_iota(jnp.int32, (tokens, kw), 0) < limit
    out[tokens + EXTRA :, :] = jnp.where(valid, keys[...], jnp.zeros_like(keys))
    kept = lax.broadcasted_iota(jnp.int32, ratios.shape, 1) < limit
    partial = jnp.sum(jnp.where(kept, ratios[...], 0.0), axis=1, keepdims=True)
    high = partial.astype(BF).astype(F32)
    middle = (partial - high).astype(BF).astype(F32)
    terms = [high, middle, partial - high - middle]
    lane = lax.broadcasted_iota(jnp.int32, (EXTRA, kw), 1)
    line = lax.broadcasted_iota(jnp.int32, (EXTRA, kw), 0)
    sums = jnp.zeros((EXTRA, kw), F32)
    own = jnp.zeros((EXTRA, kw), F32)
    for i, term in enumerate(terms):
        sums = jnp.where(lane == i, term, sums)
        own = jnp.where(lane == OWN + i, term, own)
    for i in range(4):
        sums = jnp.where(lane == 3 + i, pairs[i].astype(F32), sums)
    out[tokens : tokens + EXTRA, :] = jnp.where(line == 0, sums, 0.0).astype(BF)
    mark[...] = jnp.where(line == 0, own, 0.0).astype(BF)


def prepared(place, limits, pairs, weights, gains, keys, ratios):
    tokens, kw = keys.shape
    scalar = pl.BlockSpec(memory_space=pltpu.SMEM)
    whole = pl.BlockSpec(memory_space=pltpu.VMEM)
    return pl.pallas_call(
        prepare_kernel,
        in_specs=[scalar] * 3 + [whole] * 4,
        out_specs=[whole] * 2,
        out_shape=[
            jax.ShapeDtypeStruct((2 * tokens + EXTRA, kw), BF),
            jax.ShapeDtypeStruct((EXTRA, kw), BF),
        ],
    )(place, limits, pairs, weights, gains, keys, ratios)


def join_kernel(payload, mark, out):
    rows = out.shape[0]
    out[: rows - EXTRA, :] = payload[: rows - EXTRA, :]
    out[rows - EXTRA :, :] = payload[rows - EXTRA : rows, :] + mark[...]


def joined(payload, mark):
    rows, kw = (payload.shape[0] + EXTRA) // 2, payload.shape[1]
    whole = pl.BlockSpec(memory_space=pltpu.VMEM)
    return pl.pallas_call(
        join_kernel,
        in_specs=[whole] * 2,
        out_specs=whole,
        out_shape=jax.ShapeDtypeStruct((rows, kw), BF),
        cost_estimate=FREE,
    )(payload, mark)


def coefficients(ratios, pairs):
    signs = [1.0, 1.0, -1.0, -1.0]
    out = []
    for row in range(4):
        margin = jnp.zeros_like(ratios[0])
        for other in range(4):
            margin += jnp.where(pairs[other] == pairs[row], signs[other] * ratios[other], 0.0)
        out.append(-DPO_BETA * signs[row] / (1.0 + jnp.exp(DPO_BETA * margin)))
    return out


def coef_kernel(place, pairs, gathered, out, notes, sem):
    copy = pltpu.make_async_copy(
        gathered.at[:, pl.ds(gathered.shape[1] - EXTRA, EXTRA)], notes, sem
    )
    copy.start()
    copy.wait()
    row = place[2]
    values = jnp.sum(notes[...].astype(F32).reshape(4, -1, EXTRA, notes.shape[2]), axis=1)

    def ratios(first):
        picked = values[:, :1, first : first + 3]
        return [jnp.sum(picked[r], axis=1, keepdims=True) for r in range(4)]

    first = notes[0, :1, :16].astype(F32)
    own = coefficients(ratios(OWN), [pairs[i].astype(F32) for i in range(4)])
    following = coefficients(ratios(0), [first[:, 3 + i : 4 + i] for i in range(4)])
    lane = lax.broadcasted_iota(jnp.int32, out.shape, 1)
    result = jnp.zeros(out.shape, F32)
    for r in range(4):
        result = jnp.where(lane == lax.rem(row - r + 4, 4), own[r], result)
        result = jnp.where((lane == 4) & (row == r), following[r], result)
    out[...] = result


def coef_table(place, pairs, gathered):
    scalar = pl.BlockSpec(memory_space=pltpu.SMEM)
    return pl.pallas_call(
        coef_kernel,
        in_specs=[scalar, scalar, ANYWHERE],
        out_specs=pl.BlockSpec(memory_space=pltpu.VMEM),
        out_shape=jax.ShapeDtypeStruct((8, 128), F32),
        scratch_shapes=[
            pltpu.VMEM((gathered.shape[0], EXTRA, gathered.shape[2]), BF),
            pltpu.SemaphoreType.DMA,
        ],
        cost_estimate=FREE,
    )(place, pairs, gathered)


def finish_kernel(coefs, first, second, third, fourth, gains, weights, out, sums):
    total = first[...] * coefs[:1, :1]
    for i, wave in enumerate((second, third, fourth)):
        total += wave[...].astype(F32) * coefs[:1, i + 1 : i + 2]
    out[...] = (total * gains[...].astype(F32)).astype(BF)
    sums[...] = jnp.sum(total * weights[...].astype(F32), axis=1, keepdims=True)


def finished(coefs, waves, gains, weights):
    whole = pl.BlockSpec(memory_space=pltpu.VMEM)
    rows, kw = weights.shape
    return pl.pallas_call(
        finish_kernel,
        in_specs=[whole] * 7,
        out_specs=[whole] * 2,
        out_shape=[jax.ShapeDtypeStruct((rows, kw), BF), jax.ShapeDtypeStruct((rows, 1), F32)],
        cost_estimate=FREE,
    )(coefs, *waves, gains, weights)


ORDER = (2, 1, 3, 0)


def block_products(spot, other, hidden, keys, terms, out, sem):
    y, z = spot[1], spot[2]
    core = 1 - spot[0] if other else spot[0]
    for r in ORDER:

        def block(q, carry):
            at = lax.rem(z + q, 4) * 8 + lax.rem(y + r, 4) * 2 + core
            columns = hidden[:, pl.ds(pl.multiple_of(at * BLK, BLK), BLK)]
            terms[r, q] = lax.dot_general(
                columns, keys[...], (((0,), (0,)), ((), ())), preferred_element_type=F32
            ).astype(BF)
            return carry

        lax.fori_loop(0, 4, block, 0)
        pltpu.make_async_copy(terms.at[r], out.at[r], sem.at[r]).start()
    for r in ORDER:
        pltpu.make_async_copy(terms.at[r], out.at[r], sem.at[r]).wait()


def load(source, target, sem, parts):
    rows = source.shape[0] // parts
    copies = []
    for i in range(parts):
        at = pl.ds(i * rows, rows)
        copies.append(pltpu.make_async_copy(source.at[at], target.at[at], sem.at[i]))
        copies[-1].start()
    return copies


def send_kernel(spot, payload, hidden, *refs):
    out, keys, states, terms, in_sem, out_sem = refs
    parts = 4
    rows = states.shape[0] // parts
    for i, copy in enumerate(load(hidden, states, in_sem, parts)):
        copy.wait()

        def line(j, carry):
            at = pl.ds(pl.multiple_of(i * rows + j * 16, 16), 16)
            square = jnp.zeros((16, 512), F32)
            for c in range(0, states.shape[1], 512):
                part = states[at, c : c + 512].astype(F32)
                square = square + part * part
            inv = lax.rsqrt(jnp.sum(square, axis=1, keepdims=True) / states.shape[1] + EPS)
            from_key = pl.ds(pl.multiple_of(states.shape[0] + EXTRA + i * rows + j * 16, 16), 16)
            keys[at, :] = (payload[from_key, :].astype(F32) * inv).astype(BF)
            return carry

        lax.fori_loop(0, rows // 16, line, 0)
    block_products(spot, True, states, keys, terms, out, out_sem)


def keep_kernel(spot, keys, hidden, *refs):
    out, states, terms, in_sem, out_sem = refs
    for copy in load(hidden, states, in_sem, 4):
        copy.wait()
    block_products(spot, False, states, keys, terms, out, out_sem)


def term_call(kernel, states, kw, more):
    tokens, width = states.shape
    whole = pl.BlockSpec(memory_space=pltpu.VMEM)
    return pl.pallas_call(
        kernel,
        in_specs=[pl.BlockSpec(memory_space=pltpu.SMEM), whole, ANYWHERE],
        out_specs=[ANYWHERE] + [whole] * len(more),
        out_shape=[jax.ShapeDtypeStruct((4, 4, BLK, kw), BF)] + more,
        scratch_shapes=[
            pltpu.VMEM((tokens, width), BF),
            pltpu.VMEM((4, 4, BLK, kw), BF),
            pltpu.SemaphoreType.DMA((4,)),
            pltpu.SemaphoreType.DMA((4,)),
        ],
        compiler_params=pltpu.CompilerParams(vmem_limit_bytes=VMEM_LIMIT),
        cost_estimate=pl.CostEstimate(
            flops=tokens * width * kw, bytes_accessed=width * (tokens + kw) * 2, transcendentals=0
        ),
    )


def around(value, steps):
    return moved(value, lambda z_hi, x, z_lo, y, core: (z_hi, x, z_lo, (y + steps) % 4, core))


def along(value, steps):
    return moved(value, lambda z_hi, x, z_lo, y, core: (z_hi, x, (z_lo + steps) % 4, y, core))


def added(*parts):
    return sum(part.astype(F32) for part in parts)


def grad_kernel(payload, weights, out):
    keys = payload[payload.shape[0] - out.shape[0] :, :]
    for i in range(weights.shape[0]):
        out[:, i * BLK : (i + 1) * BLK] = lax.dot_general(
            keys, weights[i, :BLK], (((1,), (1,)), ((), ())), preferred_element_type=F32
        ).astype(BF)


def unit_grads(payload, gathered, tokens):
    count, rows, kw = gathered.shape
    step = 4
    return pl.pallas_call(
        grad_kernel,
        grid=(count // step,),
        in_specs=[
            pl.BlockSpec(payload.shape, lambda i: (0, 0)),
            pl.BlockSpec((step, rows, kw), lambda i: (i, 0, 0)),
        ],
        out_specs=pl.BlockSpec((tokens, step * BLK), lambda i: (0, i)),
        out_shape=jax.ShapeDtypeStruct((tokens, count * BLK), BF),
        compiler_params=pltpu.CompilerParams(vmem_limit_bytes=VMEM_LIMIT),
        cost_estimate=FREE,
    )(payload, gathered)


def section_kernel(near_rows, far_rows, scale, is_far, slopes, *refs):
    count = len(near_rows)
    near, far = refs[:count], refs[count : count + len(far_rows)]
    out, rows, grads, done, row_sem, grad_sem, out_sem = refs[count + len(far_rows) :]
    tokens, width = rows.shape
    group, span = 16, 512
    parts = tokens // PIECE

    def fetched(sources, sizes):
        first = 0
        for source, size in zip(sources, sizes):
            for at in range(0, size, PIECE):
                spot = (first + at) // PIECE
                pltpu.make_async_copy(
                    source.at[pl.ds(at, PIECE)], rows.at[pl.ds(first + at, PIECE)], row_sem.at[spot]
                ).start()
            first += size

    def whole(i):
        return pl.ds(pl.multiple_of(i * PIECE, PIECE), PIECE)

    for i in range(parts):
        at = pl.ds(i * PIECE, PIECE)
        pltpu.make_async_copy(slopes.at[at], grads.at[at], grad_sem.at[i]).start()

    @pl.when(is_far[0] == 1)
    def _():
        fetched(far, far_rows)

    @pl.when(is_far[0] != 1)
    def _():
        fetched(near, near_rows)

    factor = scale[:1, 4:5]

    def part(i, carry):
        at = whole(i)
        pltpu.make_async_copy(slopes.at[at], grads.at[at], grad_sem.at[i]).wait()
        pltpu.make_async_copy(slopes.at[at], rows.at[at], row_sem.at[i]).wait()
        for g in range(PIECE // group):
            line = pl.ds(pl.multiple_of(i * PIECE + g * group, group), group)
            square = jnp.zeros((group, span), F32)
            cross = jnp.zeros((group, span), F32)
            for c in range(0, width, span):
                h = rows[line, c : c + span].astype(F32)
                square = square + h * h
                cross = cross + h * grads[line, c : c + span].astype(F32)
            inv = lax.rsqrt(jnp.sum(square, axis=1, keepdims=True) / width + EPS)
            inner = jnp.sum(cross, axis=1, keepdims=True) / width * inv * factor
            ahead, back = inv * factor, inv * inv * inner
            for c in range(0, width, span):
                h = rows[line, c : c + span].astype(F32)
                u = grads[line, c : c + span].astype(F32)
                done[line, c : c + span] = (ahead * u - back * h).astype(BF)
        pltpu.make_async_copy(done.at[at], out.at[at], out_sem.at[i]).start()
        return carry

    lax.fori_loop(0, parts, part, 0)
    for i in range(parts):
        at = pl.ds(i * PIECE, PIECE)
        pltpu.make_async_copy(done.at[at], out.at[at], out_sem.at[i]).wait()


def section_grads(scale, is_far, slopes, near, far):
    tokens, width = slopes.shape
    scalar = pl.BlockSpec(memory_space=pltpu.SMEM)
    near_rows, far_rows = [v.shape[0] for v in near], [v.shape[0] for v in far]
    parts = tokens // PIECE
    return pl.pallas_call(
        functools.partial(section_kernel, near_rows, far_rows),
        in_specs=[pl.BlockSpec(memory_space=pltpu.VMEM), scalar] + [ANYWHERE] * (1 + len(near) + len(far)),
        out_specs=ANYWHERE,
        out_shape=jax.ShapeDtypeStruct((tokens, width), BF),
        scratch_shapes=[pltpu.VMEM((tokens, width), BF)] * 3
        + [pltpu.SemaphoreType.DMA((parts,))] * 3,
        compiler_params=pltpu.CompilerParams(vmem_limit_bytes=VMEM_LIMIT),
        cost_estimate=FREE,
    )(scale, is_far, slopes, *near, *far)


def on_device(hidden, norm_gain, key_weight, key_cotangent, token_logratio, lengths, pair_of_row):
    states = hidden[0]
    weights = key_weight[0]
    tokens, width = states.shape
    kw = weights.shape[1]
    section, dp = lax.axis_index("section"), lax.axis_index("dp")
    core, y, z = dp % 2, (dp // 2) % 4, dp // 8
    place = jnp.stack([core, y, z, (dp * tokens) % ROW_LEN]).astype(jnp.int32)
    gains = norm_gain[0][:, None]

    payload, mark = prepared(
        place, lengths[0], pair_of_row[0], weights, gains, key_cotangent[0], token_logratio
    )
    following = to_previous(payload)
    up, low = (1, 0), (0, 3)
    early = stepped(states[:48], up, (1, 3))
    near_last = to_previous(states[128:])
    late = stepped(states[48:128], up, (1, 3))

    send, keys = term_call(send_kernel, states, kw, [jax.ShapeDtypeStruct((tokens, kw), BF)])(
        place, payload, states
    )
    following, early = gated([following, early], [keys])
    joint = joined(following, mark)
    gathered = lax.all_gather(joint, "dp", axis=0, tiled=True)
    gathered = gathered.reshape(-1, tokens + EXTRA, kw)
    last = [stepped(early, (1, 3), low)]

    def over_cores(operands):
        states, keys, place, send, _ = operands
        swapped = moved(send, lambda z_hi, x, z_lo, y, core: (z_hi, x, z_lo, y, 1 - core))
        keep = term_call(keep_kernel, states, kw, [])(place, keys, states)[0]
        far = added(keep[2], swapped[2]).astype(BF)
        far_up, far_down = around(far[:2], 1), around(far[2:], -1)
        sums = added(keep, swapped).astype(BF)
        up_terms = jnp.concatenate([added(sums[1, :2], far_up).astype(BF), sums[1, 2:]])
        down_terms = jnp.concatenate([sums[3, :2], added(sums[3, 2:], far_down).astype(BF)])
        return sums[0], up_terms, down_terms

    def over_chips(operands):
        here, up_terms, down_terms = operands
        plane = added(here, around(up_terms, 1), around(down_terms, -1))
        first, second = along(plane[1].astype(BF), 1), along(plane[2].astype(BF), 2)
        third = gated([plane[3].astype(BF)], [first])[0]
        return plane[0], first, second, along(third, 3)

    def staged(step, operands):
        shapes = jax.eval_shape(step, operands)
        blank = lambda _: jax.tree.map(lambda v: jnp.zeros(v.shape, v.dtype), shapes)
        return lax.cond(dp < tokens, step, blank, operands)

    sums = staged(over_cores, (states, keys, place, send, joint))
    late = gated([late], [sums[0]])[0]
    last.append(stepped(late, (1, 3), low))
    near_first = lowered_part(states[:128], sums[0])
    waves = staged(over_chips, sums)

    coefs = coef_table(place, pair_of_row[0], gathered)
    weight_grad, gain_grad = finished(coefs, waves, gains, weights)

    slopes = unit_grads(following, gathered, tokens)
    is_far = (section == 3).astype(jnp.int32)[None]
    out = section_grads(coefs, is_far, slopes, [near_first, near_last], [*last, near_last])
    return out[None], weight_grad[None], gain_grad.astype(BF).reshape(1, -1)


def solution(mesh):
    in_specs = (
        P("section", "dp", None),
        P("section", "dp"),
        P("section", "dp", None),
        P("section", "dp", None),
        P("section", "dp"),
        P("section", None),
        P("section", None),
    )
    out_specs = (P("section", "dp", None), P("section", "dp", None), P("section", "dp"))
    return jax.shard_map(
        on_device, mesh=mesh, in_specs=in_specs, out_specs=out_specs, check_vma=False
    )
```

```python
import functools
import jax
import jax.numpy as jnp
from jax import lax
from jax.experimental import pallas as pl
from jax.experimental.pallas import tpu as pltpu
from jax.sharding import PartitionSpec as P

ROW_LEN = 2048
DPO_BETA = 0.1
EPS = 1e-06
AXES = ("section", "dp")
BF, F32 = jnp.bfloat16, jnp.float32
BLK = 256
PIECE = 16
FREE = pl.CostEstimate(flops=0, bytes_accessed=0, transcendentals=0)
EXTRA = 16
QUARTER = 64
OWN = 16
VMEM_LIMIT = 56 * 1024 * 1024


def index_of(z_hi, x, z_lo, y, core):
    return ((z_hi * 4 + x) * 4 + z_lo) * 8 + y * 2 + core


def moved(value, target):
    pairs = []
    for z_hi in range(2):
        for x in range(4):
            for z_lo in range(4):
                for y in range(4):
                    for core in range(2):
                        goal = target(z_hi, x, z_lo, y, core)
                        if goal is not None:
                            pairs.append((index_of(z_hi, x, z_lo, y, core), index_of(*goal)))
    return lax.ppermute(value, AXES, pairs)


def to_previous(value):
    def target(z_hi, x, z_lo, y, core):
        section = z_hi * 4 + x - 1
        return None if section < 0 else (section // 4, section % 4, z_lo, y, core)

    return moved(value, target)


ANYWHERE = pl.BlockSpec(memory_space=pl.ANY)


def gated(values, events):
    count = len(values)
    return pl.pallas_call(
        lambda *refs: None,
        in_specs=[ANYWHERE] * (count + len(events)),
        out_specs=[ANYWHERE] * count,
        out_shape=[jax.ShapeDtypeStruct(v.shape, v.dtype) for v in values],
        input_output_aliases={i: i for i in range(count)},
        cost_estimate=FREE,
    )(*values, *events)


def stepped(value, source, goal):
    return moved(
        value,
        lambda z_hi, x, z_lo, y, core: (*goal, z_lo, y, core) if (z_hi, x) == source else None,
    )


def lowered(value):
    return moved(
        value, lambda z_hi, x, z_lo, y, core: (z_hi, x - 1, z_lo, y, core) if x else None
    )


def prepare_kernel(place, limits, pairs, weights, gains, keys, ratios, out, mark):
    tokens, kw = keys.shape
    out[:tokens, :] = (weights[...].astype(F32) * gains[...].astype(F32)).astype(BF)
    limit = limits[place[2]] - place[3]
    valid = lax.broadcasted_iota(jnp.int32, (tokens, kw), 0) < limit
    out[tokens + EXTRA :, :] = jnp.where(valid, keys[...], jnp.zeros_like(keys))
    kept = lax.broadcasted_iota(jnp.int32, ratios.shape, 1) < limit
    partial = jnp.sum(jnp.where(kept, ratios[...], 0.0), axis=1, keepdims=True)
    high = partial.astype(BF).astype(F32)
    middle = (partial - high).astype(BF).astype(F32)
    terms = [high, middle, partial - high - middle]
    lane = lax.broadcasted_iota(jnp.int32, (EXTRA, kw), 1)
    line = lax.broadcasted_iota(jnp.int32, (EXTRA, kw), 0)
    sums = jnp.zeros((EXTRA, kw), F32)
    own = jnp.zeros((EXTRA, kw), F32)
    for i, term in enumerate(terms):
        sums = jnp.where(lane == i, term, sums)
        own = jnp.where(lane == OWN + i, term, own)
    for i in range(4):
        sums = jnp.where(lane == 3 + i, pairs[i].astype(F32), sums)
    out[tokens : tokens + EXTRA, :] = jnp.where(line == 0, sums, 0.0).astype(BF)
    mark[...] = jnp.where(line == 0, own, 0.0).astype(BF)


def prepared(place, limits, pairs, weights, gains, keys, ratios):
    tokens, kw = keys.shape
    scalar = pl.BlockSpec(memory_space=pltpu.SMEM)
    whole = pl.BlockSpec(memory_space=pltpu.VMEM)
    return pl.pallas_call(
        prepare_kernel,
        in_specs=[scalar] * 3 + [whole] * 4,
        out_specs=[whole] * 2,
        out_shape=[
            jax.ShapeDtypeStruct((2 * tokens + EXTRA, kw), BF),
            jax.ShapeDtypeStruct((EXTRA, kw), BF),
        ],
    )(place, limits, pairs, weights, gains, keys, ratios)


def join_kernel(payload, mark, out):
    rows = out.shape[0]
    out[: rows - EXTRA, :] = payload[: rows - EXTRA, :]
    out[rows - EXTRA :, :] = payload[rows - EXTRA : rows, :] + mark[...]


def joined(payload, mark):
    rows, kw = (payload.shape[0] + EXTRA) // 2, payload.shape[1]
    whole = pl.BlockSpec(memory_space=pltpu.VMEM)
    return pl.pallas_call(
        join_kernel,
        in_specs=[whole] * 2,
        out_specs=whole,
        out_shape=jax.ShapeDtypeStruct((rows, kw), BF),
        cost_estimate=FREE,
    )(payload, mark)


def coefficients(ratios, pairs):
    signs = [1.0, 1.0, -1.0, -1.0]
    out = []
    for row in range(4):
        margin = jnp.zeros_like(ratios[0])
        for other in range(4):
            margin += jnp.where(pairs[other] == pairs[row], signs[other] * ratios[other], 0.0)
        out.append(-DPO_BETA * signs[row] / (1.0 + jnp.exp(DPO_BETA * margin)))
    return out


def coef_kernel(place, pairs, gathered, out, notes, sem):
    copy = pltpu.make_async_copy(
        gathered.at[:, pl.ds(gathered.shape[1] - EXTRA, EXTRA)], notes, sem
    )
    copy.start()
    copy.wait()
    row = place[2]
    values = jnp.sum(notes[...].astype(F32).reshape(4, -1, EXTRA, notes.shape[2]), axis=1)

    def ratios(first):
        picked = values[:, :1, first : first + 3]
        return [jnp.sum(picked[r], axis=1, keepdims=True) for r in range(4)]

    first = notes[0, :1, :16].astype(F32)
    own = coefficients(ratios(OWN), [pairs[i].astype(F32) for i in range(4)])
    following = coefficients(ratios(0), [first[:, 3 + i : 4 + i] for i in range(4)])
    lane = lax.broadcasted_iota(jnp.int32, out.shape, 1)
    result = jnp.zeros(out.shape, F32)
    for r in range(4):
        result = jnp.where(lane == lax.rem(row - r + 4, 4), own[r], result)
        result = jnp.where((lane == 4) & (row == r), following[r], result)
    out[...] = result


def coef_table(place, pairs, gathered):
    scalar = pl.BlockSpec(memory_space=pltpu.SMEM)
    return pl.pallas_call(
        coef_kernel,
        in_specs=[scalar, scalar, ANYWHERE],
        out_specs=pl.BlockSpec(memory_space=pltpu.VMEM),
        out_shape=jax.ShapeDtypeStruct((8, 128), F32),
        scratch_shapes=[
            pltpu.VMEM((gathered.shape[0], EXTRA, gathered.shape[2]), BF),
            pltpu.SemaphoreType.DMA,
        ],
        cost_estimate=FREE,
    )(place, pairs, gathered)


def finish_kernel(coefs, first, second, third, fourth, gains, weights, out, sums):
    total = first[...] * coefs[:1, :1]
    for i, wave in enumerate((second, third, fourth)):
        total += wave[...].astype(F32) * coefs[:1, i + 1 : i + 2]
    out[...] = (total * gains[...].astype(F32)).astype(BF)
    sums[...] = jnp.sum(total * weights[...].astype(F32), axis=1, keepdims=True)


def finished(coefs, waves, gains, weights):
    whole = pl.BlockSpec(memory_space=pltpu.VMEM)
    rows, kw = weights.shape
    return pl.pallas_call(
        finish_kernel,
        in_specs=[whole] * 7,
        out_specs=[whole] * 2,
        out_shape=[jax.ShapeDtypeStruct((rows, kw), BF), jax.ShapeDtypeStruct((rows, 1), F32)],
        cost_estimate=FREE,
    )(coefs, *waves, gains, weights)


ORDER = (2, 1, 3, 0)


def block_products(spot, other, hidden, keys, terms, out, sem):
    y, z = spot[1], spot[2]
    core = 1 - spot[0] if other else spot[0]
    for r in ORDER:

        def block(q, carry):
            at = lax.rem(z + q, 4) * 8 + lax.rem(y + r, 4) * 2 + core
            columns = hidden[:, pl.ds(pl.multiple_of(at * BLK, BLK), BLK)]
            terms[r, q] = lax.dot_general(
                columns, keys[...], (((0,), (0,)), ((), ())), preferred_element_type=F32
            ).astype(BF)
            return carry

        lax.fori_loop(0, 4, block, 0)
        pltpu.make_async_copy(terms.at[r], out.at[r], sem.at[r]).start()
    for r in ORDER:
        pltpu.make_async_copy(terms.at[r], out.at[r], sem.at[r]).wait()


def load(source, target, sem, parts):
    rows = source.shape[0] // parts
    copies = []
    for i in range(parts):
        at = pl.ds(i * rows, rows)
        copies.append(pltpu.make_async_copy(source.at[at], target.at[at], sem.at[i]))
        copies[-1].start()
    return copies


def send_kernel(spot, payload, hidden, *refs):
    out, *quarters, keys, states, terms, in_sem, out_sem, row_sem = refs
    parts = 4
    rows = states.shape[0] // parts
    for i, copy in enumerate(load(hidden, states, in_sem, parts)):
        copy.wait()

        def line(j, carry):
            at = pl.ds(pl.multiple_of(i * rows + j * 16, 16), 16)
            square = jnp.zeros((16, 512), F32)
            for c in range(0, states.shape[1], 512):
                part = states[at, c : c + 512].astype(F32)
                square = square + part * part
            inv = lax.rsqrt(jnp.sum(square, axis=1, keepdims=True) / states.shape[1] + EPS)
            from_key = pl.ds(pl.multiple_of(states.shape[0] + EXTRA + i * rows + j * 16, 16), 16)
            keys[at, :] = (payload[from_key, :].astype(F32) * inv).astype(BF)
            return carry

        lax.fori_loop(0, rows // 16, line, 0)
    copies = [
        pltpu.make_async_copy(states.at[pl.ds(i * QUARTER, QUARTER)], quarter, row_sem.at[i])
        for i, quarter in enumerate(quarters)
    ]
    for copy in copies:
        copy.start()
    block_products(spot, True, states, keys, terms, out, out_sem)
    for copy in copies:
        copy.wait()


def keep_kernel(spot, keys, hidden, *refs):
    out, states, terms, in_sem, out_sem = refs
    for copy in load(hidden, states, in_sem, 4):
        copy.wait()
    block_products(spot, False, states, keys, terms, out, out_sem)


def term_call(kernel, operands, more):
    tokens, width = operands[2].shape
    kw = operands[1].shape[1]
    whole = pl.BlockSpec(memory_space=pltpu.VMEM)
    rows = [jax.ShapeDtypeStruct((QUARTER, width), BF)] * 4
    keys = jax.ShapeDtypeStruct((tokens, kw), BF)
    return pl.pallas_call(
        kernel,
        in_specs=[pl.BlockSpec(memory_space=pltpu.SMEM), whole, ANYWHERE],
        out_specs=[ANYWHERE] + ([ANYWHERE] * 4 + [whole] if more else []),
        out_shape=[jax.ShapeDtypeStruct((4, 4, BLK, kw), BF)] + ([*rows, keys] if more else []),
        scratch_shapes=[
            pltpu.VMEM((tokens, width), BF),
            pltpu.VMEM((4, 4, BLK, kw), BF),
            pltpu.SemaphoreType.DMA((4,)),
            pltpu.SemaphoreType.DMA((4,)),
        ]
        + ([pltpu.SemaphoreType.DMA((4,))] if more else []),
        compiler_params=pltpu.CompilerParams(vmem_limit_bytes=VMEM_LIMIT),
        cost_estimate=FREE,
    )(*operands)


def around(value, steps):
    return moved(value, lambda z_hi, x, z_lo, y, core: (z_hi, x, z_lo, (y + steps) % 4, core))


def along(value, steps):
    return moved(value, lambda z_hi, x, z_lo, y, core: (z_hi, x, (z_lo + steps) % 4, y, core))


def added(*parts):
    return sum(part.astype(F32) for part in parts)


def grad_kernel(payload, weights, out):
    keys = payload[payload.shape[0] - out.shape[0] :, :]
    for i in range(weights.shape[0]):
        out[:, i * BLK : (i + 1) * BLK] = lax.dot_general(
            keys, weights[i, :BLK], (((1,), (1,)), ((), ())), preferred_element_type=F32
        ).astype(BF)


def unit_grads(payload, gathered, tokens):
    count, rows, kw = gathered.shape
    step = 4
    return pl.pallas_call(
        grad_kernel,
        grid=(count // step,),
        in_specs=[
            pl.BlockSpec(payload.shape, lambda i: (0, 0)),
            pl.BlockSpec((step, rows, kw), lambda i: (i, 0, 0)),
        ],
        out_specs=pl.BlockSpec((tokens, step * BLK), lambda i: (0, i)),
        out_shape=jax.ShapeDtypeStruct((tokens, count * BLK), BF),
        compiler_params=pltpu.CompilerParams(vmem_limit_bytes=VMEM_LIMIT),
        cost_estimate=FREE,
    )(payload, gathered)


def section_kernel(near_rows, far_rows, scale, is_far, slopes, *refs):
    count = len(near_rows)
    near, far = refs[:count], refs[count : count + len(far_rows)]
    out, rows, grads, done, row_sem, grad_sem, out_sem = refs[count + len(far_rows) :]
    tokens, width = rows.shape
    group, span = 16, 512
    parts = tokens // PIECE

    def fetched(sources, sizes):
        first = 0
        for source, size in zip(sources, sizes):
            for at in range(0, size, PIECE):
                spot = (first + at) // PIECE
                pltpu.make_async_copy(
                    source.at[pl.ds(at, PIECE)], rows.at[pl.ds(first + at, PIECE)], row_sem.at[spot]
                ).start()
            first += size

    def whole(i):
        return pl.ds(pl.multiple_of(i * PIECE, PIECE), PIECE)

    for i in range(parts):
        at = pl.ds(i * PIECE, PIECE)
        pltpu.make_async_copy(slopes.at[at], grads.at[at], grad_sem.at[i]).start()

    @pl.when(is_far[0] == 1)
    def _():
        fetched(far, far_rows)

    @pl.when(is_far[0] != 1)
    def _():
        fetched(near, near_rows)

    factor = scale[:1, 4:5]

    def part(i, carry):
        at = whole(i)
        pltpu.make_async_copy(slopes.at[at], grads.at[at], grad_sem.at[i]).wait()
        pltpu.make_async_copy(slopes.at[at], rows.at[at], row_sem.at[i]).wait()
        for g in range(PIECE // group):
            line = pl.ds(pl.multiple_of(i * PIECE + g * group, group), group)
            square = jnp.zeros((group, span), F32)
            cross = jnp.zeros((group, span), F32)
            for c in range(0, width, span):
                h = rows[line, c : c + span].astype(F32)
                square = square + h * h
                cross = cross + h * grads[line, c : c + span].astype(F32)
            inv = lax.rsqrt(jnp.sum(square, axis=1, keepdims=True) / width + EPS)
            inner = jnp.sum(cross, axis=1, keepdims=True) / width * inv * factor
            ahead, back = inv * factor, inv * inv * inner
            for c in range(0, width, span):
                h = rows[line, c : c + span].astype(F32)
                u = grads[line, c : c + span].astype(F32)
                done[line, c : c + span] = (ahead * u - back * h).astype(BF)
        pltpu.make_async_copy(done.at[at], out.at[at], out_sem.at[i]).start()
        return carry

    lax.fori_loop(0, parts, part, 0)
    for i in range(parts):
        at = pl.ds(i * PIECE, PIECE)
        pltpu.make_async_copy(done.at[at], out.at[at], out_sem.at[i]).wait()


def section_grads(scale, is_far, slopes, near, far):
    tokens, width = slopes.shape
    scalar = pl.BlockSpec(memory_space=pltpu.SMEM)
    near_rows, far_rows = [v.shape[0] for v in near], [v.shape[0] for v in far]
    parts = tokens // PIECE
    return pl.pallas_call(
        functools.partial(section_kernel, near_rows, far_rows),
        in_specs=[pl.BlockSpec(memory_space=pltpu.VMEM), scalar] + [ANYWHERE] * (1 + len(near) + len(far)),
        out_specs=ANYWHERE,
        out_shape=jax.ShapeDtypeStruct((tokens, width), BF),
        scratch_shapes=[pltpu.VMEM((tokens, width), BF)] * 3
        + [pltpu.SemaphoreType.DMA((parts,))] * 3,
        compiler_params=pltpu.CompilerParams(vmem_limit_bytes=VMEM_LIMIT),
        cost_estimate=FREE,
    )(scale, is_far, slopes, *near, *far)


def on_device(hidden, norm_gain, key_weight, key_cotangent, token_logratio, lengths, pair_of_row):
    states = hidden[0]
    weights = key_weight[0]
    tokens, width = states.shape
    kw = weights.shape[1]
    section, dp = lax.axis_index("section"), lax.axis_index("dp")
    core, y, z = dp % 2, (dp // 2) % 4, dp // 8
    place = jnp.stack([core, y, z, (dp * tokens) % ROW_LEN]).astype(jnp.int32)
    gains = norm_gain[0][:, None]

    payload, mark = prepared(
        place, lengths[0], pair_of_row[0], weights, gains, key_cotangent[0], token_logratio
    )
    following = to_previous(payload)

    send, *quarters, keys = term_call(send_kernel, (place, payload, states), True)
    following = gated([following], [keys])[0]
    joint = joined(following, mark)
    send = gated([send], [joint])[0]
    gathered = lax.all_gather(joint, "dp", axis=0, tiled=True)
    gathered = gathered.reshape(-1, tokens + EXTRA, kw)
    near = lowered(states)
    up = (1, 0)
    spread = [stepped(quarter, up, (1, x + 1)) for x, quarter in enumerate(quarters[1:])]

    def over_cores(operands):
        states, keys, place, send = operands
        swapped = moved(send, lambda z_hi, x, z_lo, y, core: (z_hi, x, z_lo, y, 1 - core))
        keep = term_call(keep_kernel, (place, keys, states), False)[0]
        return added(keep, swapped).astype(BF)

    def over_far_chips(operands):
        sums = operands
        far_up, far_down = around(sums[2, :2], 1), around(sums[2, 2:], -1)
        up_terms = jnp.concatenate([added(sums[1, :2], far_up).astype(BF), sums[1, 2:]])
        down_terms = jnp.concatenate([sums[3, :2], added(sums[3, 2:], far_down).astype(BF)])
        return sums[0], up_terms, down_terms

    def over_chips(operands):
        here, up_terms, down_terms = operands
        plane = added(here, around(up_terms, 1), around(down_terms, -1))
        return plane[0], plane[1].astype(BF), plane[2].astype(BF), plane[3].astype(BF)

    def staged(step, operands):
        shapes = jax.eval_shape(step, operands)
        blank = lambda _: jax.tree.map(lambda v: jnp.zeros(v.shape, v.dtype), shapes)
        return lax.cond(dp < tokens, step, blank, operands)

    sums = staged(over_cores, (states, keys, place, send))
    spread = gated(spread, [sums])
    crossing = jnp.where(section == 4, quarters[0], sum(spread))
    crossed = moved(
        crossing, lambda z_hi, x, z_lo, y, core: (0, x, z_lo, y, core) if z_hi else None
    )
    plane = staged(over_chips, staged(over_far_chips, sums))
    waves = [plane[0], *[along(wave, i + 1) for i, wave in enumerate(plane[1:])]]

    crossed = gated([crossed], plane[:1])[0]
    far = [stepped(crossed, (0, x), (0, 3)) for x in range(3)] + [crossed]

    coefs = coef_table(place, pair_of_row[0], gathered)
    weight_grad, gain_grad = finished(coefs, waves, gains, weights)

    slopes = unit_grads(following, gathered, tokens)
    is_far = (section == 3).astype(jnp.int32)[None]
    out = section_grads(coefs, is_far, slopes, [near], far)
    return out[None], weight_grad[None], gain_grad.astype(BF).reshape(1, -1)


def solution(mesh):
    in_specs = (
        P("section", "dp", None),
        P("section", "dp"),
        P("section", "dp", None),
        P("section", "dp", None),
        P("section", "dp"),
        P("section", None),
        P("section", None),
    )
    out_specs = (P("section", "dp", None), P("section", "dp", None), P("section", "dp"))
    return jax.shard_map(
        on_device, mesh=mesh, in_specs=in_specs, out_specs=out_specs, check_vma=False
    )
```

```python
import functools
import jax
import jax.numpy as jnp
from jax import lax
from jax.experimental import pallas as pl
from jax.experimental.pallas import tpu as pltpu
from jax.sharding import PartitionSpec as P

ROW_LEN = 2048
DPO_BETA = 0.1
EPS = 1e-06
AXES = ("section", "dp")
BF, F32 = jnp.bfloat16, jnp.float32
BLK = 256
PIECE = 16
FREE = pl.CostEstimate(flops=0, bytes_accessed=0, transcendentals=0)
EXTRA = 16
QUARTER = 64
OWN = 16
VMEM_LIMIT = 56 * 1024 * 1024


def index_of(z_hi, x, z_lo, y, core):
    return ((z_hi * 4 + x) * 4 + z_lo) * 8 + y * 2 + core


def moved(value, target):
    pairs = []
    for z_hi in range(2):
        for x in range(4):
            for z_lo in range(4):
                for y in range(4):
                    for core in range(2):
                        goal = target(z_hi, x, z_lo, y, core)
                        if goal is not None:
                            pairs.append((index_of(z_hi, x, z_lo, y, core), index_of(*goal)))
    return lax.ppermute(value, AXES, pairs)


def to_previous(value):
    def target(z_hi, x, z_lo, y, core):
        section = z_hi * 4 + x - 1
        return None if section < 0 else (section // 4, section % 4, z_lo, y, core)

    return moved(value, target)


ANYWHERE = pl.BlockSpec(memory_space=pl.ANY)


def gated(values, events):
    count = len(values)
    return pl.pallas_call(
        lambda *refs: None,
        in_specs=[ANYWHERE] * (count + len(events)),
        out_specs=[ANYWHERE] * count,
        out_shape=[jax.ShapeDtypeStruct(v.shape, v.dtype) for v in values],
        input_output_aliases={i: i for i in range(count)},
        cost_estimate=FREE,
    )(*values, *events)


def stepped(value, source, goal):
    return moved(
        value,
        lambda z_hi, x, z_lo, y, core: (*goal, z_lo, y, core) if (z_hi, x) == source else None,
    )


def lowered(value):
    return moved(
        value, lambda z_hi, x, z_lo, y, core: (z_hi, x - 1, z_lo, y, core) if x else None
    )


def picked_kernel(section, *refs):
    *sources, out, held, sem = refs
    for i, source in enumerate(sources):

        @pl.when(section[0] == 5 + i)
        def _():
            for start, end in ((source, held), (held, out)):
                copy = pltpu.make_async_copy(start, end, sem)
                copy.start()
                copy.wait()


def picked(section, sources):
    shape = sources[0].shape
    return pl.pallas_call(
        picked_kernel,
        in_specs=[pl.BlockSpec(memory_space=pltpu.SMEM)] + [ANYWHERE] * 3,
        out_specs=ANYWHERE,
        out_shape=jax.ShapeDtypeStruct(shape, BF),
        scratch_shapes=[pltpu.VMEM(shape, BF), pltpu.SemaphoreType.DMA],
        compiler_params=pltpu.CompilerParams(vmem_limit_bytes=VMEM_LIMIT),
        cost_estimate=FREE,
    )(section[None], *sources)


def prepare_kernel(place, limits, pairs, weights, gains, keys, ratios, out, mark):
    tokens, kw = keys.shape
    out[:tokens, :] = (weights[...].astype(F32) * gains[...].astype(F32)).astype(BF)
    limit = limits[place[2]] - place[3]
    valid = lax.broadcasted_iota(jnp.int32, (tokens, kw), 0) < limit
    out[tokens + EXTRA :, :] = jnp.where(valid, keys[...], jnp.zeros_like(keys))
    kept = lax.broadcasted_iota(jnp.int32, ratios.shape, 1) < limit
    partial = jnp.sum(jnp.where(kept, ratios[...], 0.0), axis=1, keepdims=True)
    high = partial.astype(BF).astype(F32)
    middle = (partial - high).astype(BF).astype(F32)
    terms = [high, middle, partial - high - middle]
    lane = lax.broadcasted_iota(jnp.int32, (EXTRA, kw), 1)
    line = lax.broadcasted_iota(jnp.int32, (EXTRA, kw), 0)
    sums = jnp.zeros((EXTRA, kw), F32)
    own = jnp.zeros((EXTRA, kw), F32)
    for i, term in enumerate(terms):
        sums = jnp.where(lane == i, term, sums)
        own = jnp.where(lane == OWN + i, term, own)
    for i in range(4):
        sums = jnp.where(lane == 3 + i, pairs[i].astype(F32), sums)
    out[tokens : tokens + EXTRA, :] = jnp.where(line == 0, sums, 0.0).astype(BF)
    mark[...] = jnp.where(line == 0, own, 0.0).astype(BF)


def prepared(place, limits, pairs, weights, gains, keys, ratios):
    tokens, kw = keys.shape
    scalar = pl.BlockSpec(memory_space=pltpu.SMEM)
    whole = pl.BlockSpec(memory_space=pltpu.VMEM)
    return pl.pallas_call(
        prepare_kernel,
        in_specs=[scalar] * 3 + [whole] * 4,
        out_specs=[whole] * 2,
        out_shape=[
            jax.ShapeDtypeStruct((2 * tokens + EXTRA, kw), BF),
            jax.ShapeDtypeStruct((EXTRA, kw), BF),
        ],
    )(place, limits, pairs, weights, gains, keys, ratios)


def join_kernel(payload, mark, out):
    rows = out.shape[0]
    out[: rows - EXTRA, :] = payload[: rows - EXTRA, :]
    out[rows - EXTRA :, :] = payload[rows - EXTRA : rows, :] + mark[...]


def joined(payload, mark):
    rows, kw = (payload.shape[0] + EXTRA) // 2, payload.shape[1]
    whole = pl.BlockSpec(memory_space=pltpu.VMEM)
    return pl.pallas_call(
        join_kernel,
        in_specs=[whole] * 2,
        out_specs=whole,
        out_shape=jax.ShapeDtypeStruct((rows, kw), BF),
        cost_estimate=FREE,
    )(payload, mark)


def coefficients(ratios, pairs):
    signs = [1.0, 1.0, -1.0, -1.0]
    out = []
    for row in range(4):
        margin = jnp.zeros_like(ratios[0])
        for other in range(4):
            margin += jnp.where(pairs[other] == pairs[row], signs[other] * ratios[other], 0.0)
        out.append(-DPO_BETA * signs[row] / (1.0 + jnp.exp(DPO_BETA * margin)))
    return out


def coef_kernel(place, pairs, gathered, out, notes, sem):
    copy = pltpu.make_async_copy(
        gathered.at[:, pl.ds(gathered.shape[1] - EXTRA, EXTRA), pl.ds(0, 128)], notes, sem
    )
    copy.start()
    copy.wait()
    row = place[2]
    values = jnp.sum(notes[...].astype(F32).reshape(4, -1, EXTRA, notes.shape[2]), axis=1)

    def ratios(first):
        picked = values[:, :1, first : first + 3]
        return [jnp.sum(picked[r], axis=1, keepdims=True) for r in range(4)]

    first = notes[0, :1, :16].astype(F32)
    own = coefficients(ratios(OWN), [pairs[i].astype(F32) for i in range(4)])
    following = coefficients(ratios(0), [first[:, 3 + i : 4 + i] for i in range(4)])
    lane = lax.broadcasted_iota(jnp.int32, out.shape, 1)
    result = jnp.zeros(out.shape, F32)
    for r in range(4):
        result = jnp.where(lane == lax.rem(row - r + 4, 4), own[r], result)
        result = jnp.where((lane == 4) & (row == r), following[r], result)
    out[...] = result


def coef_table(place, pairs, gathered):
    scalar = pl.BlockSpec(memory_space=pltpu.SMEM)
    return pl.pallas_call(
        coef_kernel,
        in_specs=[scalar, scalar, ANYWHERE],
        out_specs=pl.BlockSpec(memory_space=pltpu.VMEM),
        out_shape=jax.ShapeDtypeStruct((8, 128), F32),
        scratch_shapes=[
            pltpu.VMEM((gathered.shape[0], EXTRA, 128), BF),
            pltpu.SemaphoreType.DMA,
        ],
        cost_estimate=FREE,
    )(place, pairs, gathered)


def finish_kernel(coefs, first, second, third, fourth, gains, weights, out, sums):
    total = first[...] * coefs[:1, :1]
    for i, wave in enumerate((second, third, fourth)):
        total += wave[...].astype(F32) * coefs[:1, i + 1 : i + 2]
    out[...] = (total * gains[...].astype(F32)).astype(BF)
    found = jnp.sum(total * weights[...].astype(F32), axis=1, keepdims=True)
    sums[...] = jnp.broadcast_to(found, (found.shape[0], 128)).T[:1].astype(BF)


def finished(coefs, waves, gains, weights):
    whole = pl.BlockSpec(memory_space=pltpu.VMEM)
    rows, kw = weights.shape
    return pl.pallas_call(
        finish_kernel,
        in_specs=[whole] * 7,
        out_specs=[whole] * 2,
        out_shape=[jax.ShapeDtypeStruct((rows, kw), BF), jax.ShapeDtypeStruct((1, rows), BF)],
        cost_estimate=FREE,
    )(coefs, *waves, gains, weights)


ORDER = (2, 1, 3, 0)


def block_products(spot, other, hidden, keys, terms, out, sem):
    y, z = spot[1], spot[2]
    core = 1 - spot[0] if other else spot[0]
    for r in ORDER:

        def block(q, carry):
            at = lax.rem(z + q, 4) * 8 + lax.rem(y + r, 4) * 2 + core
            columns = hidden[:, pl.ds(pl.multiple_of(at * BLK, BLK), BLK)]
            terms[r, q] = lax.dot_general(
                columns, keys[...], (((0,), (0,)), ((), ())), preferred_element_type=F32
            ).astype(BF)
            return carry

        lax.fori_loop(0, 4, block, 0)
        pltpu.make_async_copy(terms.at[r], out.at[r], sem.at[r]).start()
    for r in ORDER:
        pltpu.make_async_copy(terms.at[r], out.at[r], sem.at[r]).wait()


def load(source, target, sem, parts):
    rows = source.shape[0] // parts
    copies = []
    for i in range(parts):
        at = pl.ds(i * rows, rows)
        copies.append(pltpu.make_async_copy(source.at[at], target.at[at], sem.at[i]))
        copies[-1].start()
    return copies


def send_kernel(spot, payload, hidden, *refs):
    out, *quarters, keys, states, terms, in_sem, out_sem, row_sem = refs
    parts = 4
    rows = states.shape[0] // parts
    for i, copy in enumerate(load(hidden, states, in_sem, parts)):
        copy.wait()

        def line(j, carry):
            at = pl.ds(pl.multiple_of(i * rows + j * 16, 16), 16)
            square = jnp.zeros((16, 512), F32)
            for c in range(0, states.shape[1], 512):
                part = states[at, c : c + 512].astype(F32)
                square = square + part * part
            inv = lax.rsqrt(jnp.sum(square, axis=1, keepdims=True) / states.shape[1] + EPS)
            from_key = pl.ds(pl.multiple_of(states.shape[0] + EXTRA + i * rows + j * 16, 16), 16)
            keys[at, :] = (payload[from_key, :].astype(F32) * inv).astype(BF)
            return carry

        lax.fori_loop(0, rows // 16, line, 0)
    copies = [
        pltpu.make_async_copy(states.at[pl.ds(i * QUARTER, QUARTER)], quarter, row_sem.at[i])
        for i, quarter in enumerate(quarters)
    ]
    for copy in copies:
        copy.start()
    block_products(spot, True, states, keys, terms, out, out_sem)
    for copy in copies:
        copy.wait()


def keep_kernel(spot, keys, hidden, *refs):
    out, states, terms, in_sem, out_sem, _ = refs
    for copy in load(hidden, states, in_sem, 4):
        copy.wait()
    block_products(spot, False, states, keys, terms, out, out_sem)


def term_call(kernel, operands, sending):
    tokens, width = operands[2].shape
    kw = operands[1].shape[1]
    whole = pl.BlockSpec(memory_space=pltpu.VMEM)
    more = [jax.ShapeDtypeStruct((QUARTER, width), BF)] * 4 if sending else []
    keys = [jax.ShapeDtypeStruct((tokens, kw), BF)] if sending else []
    return pl.pallas_call(
        kernel,
        in_specs=[pl.BlockSpec(memory_space=pltpu.SMEM), whole, ANYWHERE],
        out_specs=[ANYWHERE] * (1 + len(more)) + [whole] * len(keys),
        out_shape=[jax.ShapeDtypeStruct((4, 4, BLK, kw), BF), *more, *keys],
        scratch_shapes=[
            pltpu.VMEM((tokens, width), BF),
            pltpu.VMEM((4, 4, BLK, kw), BF),
            pltpu.SemaphoreType.DMA((4,)),
            pltpu.SemaphoreType.DMA((4,)),
            pltpu.SemaphoreType.DMA((4,)),
        ],
        compiler_params=pltpu.CompilerParams(vmem_limit_bytes=VMEM_LIMIT),
        cost_estimate=FREE,
    )(*operands)


def around(value, steps):
    return moved(value, lambda z_hi, x, z_lo, y, core: (z_hi, x, z_lo, (y + steps) % 4, core))


def along(value, steps):
    return moved(value, lambda z_hi, x, z_lo, y, core: (z_hi, x, (z_lo + steps) % 4, y, core))


def added(*parts):
    return sum(part.astype(F32) for part in parts)


def grad_kernel(payload, weights, out):
    keys = payload[payload.shape[0] - out.shape[0] :, :]
    for i in range(weights.shape[0]):
        out[:, i * BLK : (i + 1) * BLK] = lax.dot_general(
            keys, weights[i, :BLK], (((1,), (1,)), ((), ())), preferred_element_type=F32
        ).astype(BF)


def unit_grads(payload, gathered, tokens):
    count, rows, kw = gathered.shape
    step = 4
    return pl.pallas_call(
        grad_kernel,
        grid=(count // step,),
        in_specs=[
            pl.BlockSpec(payload.shape, lambda i: (0, 0)),
            pl.BlockSpec((step, rows, kw), lambda i: (i, 0, 0)),
        ],
        out_specs=pl.BlockSpec((tokens, step * BLK), lambda i: (0, i)),
        out_shape=jax.ShapeDtypeStruct((tokens, count * BLK), BF),
        compiler_params=pltpu.CompilerParams(vmem_limit_bytes=VMEM_LIMIT),
        cost_estimate=FREE,
    )(payload, gathered)


def section_kernel(near_rows, far_rows, scale, is_far, slopes, *refs):
    count = len(near_rows)
    near, far = refs[:count], refs[count : count + len(far_rows)]
    out, rows, grads, done, row_sem, grad_sem, out_sem = refs[count + len(far_rows) :]
    tokens, width = rows.shape
    group, span = 16, 512
    parts = tokens // PIECE

    def fetched(sources, sizes):
        first = 0
        for source, size in zip(sources, sizes):
            for at in range(0, size, PIECE):
                spot = (first + at) // PIECE
                pltpu.make_async_copy(
                    source.at[pl.ds(at, PIECE)], rows.at[pl.ds(first + at, PIECE)], row_sem.at[spot]
                ).start()
            first += size

    def whole(i):
        return pl.ds(pl.multiple_of(i * PIECE, PIECE), PIECE)

    for i in range(parts):
        at = pl.ds(i * PIECE, PIECE)
        pltpu.make_async_copy(slopes.at[at], grads.at[at], grad_sem.at[i]).start()

    @pl.when(is_far[0] == 1)
    def _():
        fetched(far, far_rows)

    @pl.when(is_far[0] != 1)
    def _():
        fetched(near, near_rows)

    factor = scale[:1, 4:5]

    def part(i, carry):
        at = whole(i)
        pltpu.make_async_copy(slopes.at[at], grads.at[at], grad_sem.at[i]).wait()
        pltpu.make_async_copy(slopes.at[at], rows.at[at], row_sem.at[i]).wait()
        for g in range(PIECE // group):
            line = pl.ds(pl.multiple_of(i * PIECE + g * group, group), group)
            square = jnp.zeros((group, span), F32)
            cross = jnp.zeros((group, span), F32)
            for c in range(0, width, span):
                h = rows[line, c : c + span].astype(F32)
                square = square + h * h
                cross = cross + h * grads[line, c : c + span].astype(F32)
            inv = lax.rsqrt(jnp.sum(square, axis=1, keepdims=True) / width + EPS)
            inner = jnp.sum(cross, axis=1, keepdims=True) / width * inv * factor
            ahead, back = inv * factor, inv * inv * inner
            for c in range(0, width, span):
                h = rows[line, c : c + span].astype(F32)
                u = grads[line, c : c + span].astype(F32)
                done[line, c : c + span] = (ahead * u - back * h).astype(BF)
        pltpu.make_async_copy(done.at[at], out.at[at], out_sem.at[i]).start()
        return carry

    lax.fori_loop(0, parts, part, 0)
    for i in range(parts):
        at = pl.ds(i * PIECE, PIECE)
        pltpu.make_async_copy(done.at[at], out.at[at], out_sem.at[i]).wait()


def section_grads(scale, is_far, slopes, near, far):
    tokens, width = slopes.shape
    scalar = pl.BlockSpec(memory_space=pltpu.SMEM)
    near_rows, far_rows = [v.shape[0] for v in near], [v.shape[0] for v in far]
    parts = tokens // PIECE
    return pl.pallas_call(
        functools.partial(section_kernel, near_rows, far_rows),
        in_specs=[pl.BlockSpec(memory_space=pltpu.VMEM), scalar] + [ANYWHERE] * (1 + len(near) + len(far)),
        out_specs=ANYWHERE,
        out_shape=jax.ShapeDtypeStruct((tokens, width), BF),
        scratch_shapes=[pltpu.VMEM((tokens, width), BF)] * 3
        + [pltpu.SemaphoreType.DMA((parts,))] * 3,
        compiler_params=pltpu.CompilerParams(vmem_limit_bytes=VMEM_LIMIT),
        cost_estimate=FREE,
    )(scale, is_far, slopes, *near, *far)


def on_device(hidden, norm_gain, key_weight, key_cotangent, token_logratio, lengths, pair_of_row):
    states = hidden[0]
    weights = key_weight[0]
    tokens, width = states.shape
    kw = weights.shape[1]
    section, dp = lax.axis_index("section"), lax.axis_index("dp")
    core, y, z = dp % 2, (dp // 2) % 4, dp // 8
    place = jnp.stack([core, y, z, (dp * tokens) % ROW_LEN]).astype(jnp.int32)
    gains = norm_gain[0][:, None]

    payload, mark = prepared(
        place, lengths[0], pair_of_row[0], weights, gains, key_cotangent[0], token_logratio
    )
    following = to_previous(payload)

    send, *quarters, keys = term_call(send_kernel, (place, payload, states), True)
    following = gated([following], [keys])[0]
    joint = joined(following, mark)
    send = gated([send], [joint])[0]
    gathered = lax.all_gather(joint, "dp", axis=0, tiled=True)
    gathered = gathered.reshape(-1, tokens + EXTRA, kw)
    near = lowered(states)
    up = (1, 0)
    direct = stepped(quarters[0], up, (0, 3))
    spread = {x: stepped(quarters[x], up, (1, x)) for x in (2, 3, 1)}

    def over_cores(operands):
        states, keys, place, send = operands
        swapped = moved(send, lambda z_hi, x, z_lo, y, core: (z_hi, x, z_lo, y, 1 - core))
        return swapped, *term_call(keep_kernel, (place, keys, states), False)

    def over_far_chips(operands):
        swapped, keep = operands
        sums = lambda r, *more: added(keep[r], swapped[r], *more)
        far = sums(2).astype(BF)
        far_up, far_down = around(far[:2], 1), around(far[2:], -1)
        up_terms = jnp.concatenate([far_up.astype(F32), jnp.zeros(far_up.shape, F32)])
        down_terms = jnp.concatenate([jnp.zeros(far_down.shape, F32), far_down.astype(F32)])
        return sums(0).astype(BF), sums(1, up_terms).astype(BF), sums(3, down_terms).astype(BF)

    def over_chips(operands):
        here, up_terms, down_terms = operands
        plane = added(here, around(up_terms, 1), around(down_terms, -1))
        return plane[0], *[plane[i].astype(BF) for i in (1, 2, 3)]

    def staged(step, operands):
        shapes = jax.eval_shape(step, operands)
        blank = lambda _: jax.tree.map(lambda v: jnp.zeros(v.shape, v.dtype), shapes)
        return lax.cond(dp < tokens, step, blank, operands)

    sums = staged(over_cores, (states, keys, place, send))
    second, third, first = gated([spread[x] for x in (2, 3, 1)], sums[:1])
    crossing = picked(section, [first, second, third])
    crossed = moved(
        crossing, lambda z_hi, x, z_lo, y, core: (0, x, z_lo, y, core) if z_hi and x else None
    )
    plane = staged(over_chips, staged(over_far_chips, sums))
    crossed = gated([crossed], plane[:1])[0]
    far = [direct, *[stepped(crossed, (0, x), (0, 3)) for x in (1, 2)], crossed]
    slopes = unit_grads(following, gathered, tokens)
    coefs = coef_table(place, pair_of_row[0], gathered)
    later = gated(plane[1:], [near])
    waves = [plane[0], *[along(wave, i + 1) for i, wave in enumerate(later)]]
    weight_grad, gain_grad = finished(coefs, waves, gains, weights)

    is_far = (section == 3).astype(jnp.int32)[None]
    out = section_grads(coefs, is_far, slopes, [near], far)
    return out[None], weight_grad[None], gain_grad


def solution(mesh):
    in_specs = (
        P("section", "dp", None),
        P("section", "dp"),
        P("section", "dp", None),
        P("section", "dp", None),
        P("section", "dp"),
        P("section", None),
        P("section", None),
    )
    out_specs = (P("section", "dp", None), P("section", "dp", None), P("section", "dp"))
    return jax.shard_map(
        on_device, mesh=mesh, in_specs=in_specs, out_specs=out_specs, check_vma=False
    )
```

```python
import functools
import jax
import jax.numpy as jnp
from jax import lax
from jax.experimental import pallas as pl
from jax.experimental.pallas import tpu as pltpu
from jax.sharding import PartitionSpec as P

ROW_LEN = 2048
DPO_BETA = 0.1
EPS = 1e-06
AXES = ("section", "dp")
BF, F32 = jnp.bfloat16, jnp.float32
BLK = 256
PIECE = 64
FREE = pl.CostEstimate(flops=0, bytes_accessed=0, transcendentals=0)
EXTRA = 16
QUARTER = 64
OWN = 16
VMEM_LIMIT = 56 * 1024 * 1024


def index_of(z_hi, x, z_lo, y, core):
    return ((z_hi * 4 + x) * 4 + z_lo) * 8 + y * 2 + core


def moved(value, target):
    pairs = []
    for z_hi in range(2):
        for x in range(4):
            for z_lo in range(4):
                for y in range(4):
                    for core in range(2):
                        goal = target(z_hi, x, z_lo, y, core)
                        if goal is not None:
                            pairs.append((index_of(z_hi, x, z_lo, y, core), index_of(*goal)))
    return lax.ppermute(value, AXES, pairs)


def to_previous(value):
    def target(z_hi, x, z_lo, y, core):
        section = z_hi * 4 + x - 1
        return None if section < 0 else (section // 4, section % 4, z_lo, y, core)

    return moved(value, target)


ANYWHERE = pl.BlockSpec(memory_space=pl.ANY)


def gated(values, events):
    count = len(values)
    return pl.pallas_call(
        lambda *refs: None,
        in_specs=[ANYWHERE] * (count + len(events)),
        out_specs=[ANYWHERE] * count,
        out_shape=[jax.ShapeDtypeStruct(v.shape, v.dtype) for v in values],
        input_output_aliases={i: i for i in range(count)},
        cost_estimate=FREE,
    )(*values, *events)


def stepped(value, source, goal):
    return moved(
        value,
        lambda z_hi, x, z_lo, y, core: (*goal, z_lo, y, core) if (z_hi, x) == source else None,
    )


def lowered(value):
    return moved(
        value, lambda z_hi, x, z_lo, y, core: (z_hi, x - 1, z_lo, y, core) if x else None
    )


def picked_kernel(section, *refs):
    *sources, out, held, sem = refs
    for i, source in enumerate(sources):

        @pl.when(section[0] == 5 + i)
        def _():
            for start, end in ((source, held), (held, out)):
                copy = pltpu.make_async_copy(start, end, sem)
                copy.start()
                copy.wait()


def picked(section, sources):
    shape = sources[0].shape
    return pl.pallas_call(
        picked_kernel,
        in_specs=[pl.BlockSpec(memory_space=pltpu.SMEM)] + [ANYWHERE] * 3,
        out_specs=ANYWHERE,
        out_shape=jax.ShapeDtypeStruct(shape, BF),
        scratch_shapes=[pltpu.VMEM(shape, BF), pltpu.SemaphoreType.DMA],
        compiler_params=pltpu.CompilerParams(vmem_limit_bytes=VMEM_LIMIT),
        cost_estimate=FREE,
    )(section[None], *sources)


def as_column(row):
    return jnp.broadcast_to(row.astype(F32), (128, row.shape[1])).T[:, :1]


def prepare_kernel(place, limits, pairs, weights, gains, keys, ratios, out, mark):
    tokens, kw = keys.shape
    out[:tokens, :] = (weights[...].astype(F32) * as_column(gains[...])).astype(BF)
    limit = limits[place[2]] - place[3]
    valid = lax.broadcasted_iota(jnp.int32, (tokens, kw), 0) < limit
    out[tokens + EXTRA :, :] = jnp.where(valid, keys[...], jnp.zeros_like(keys))
    kept = lax.broadcasted_iota(jnp.int32, ratios.shape, 1) < limit
    partial = jnp.sum(jnp.where(kept, ratios[...], 0.0), axis=1, keepdims=True)
    high = partial.astype(BF).astype(F32)
    middle = (partial - high).astype(BF).astype(F32)
    terms = [high, middle, partial - high - middle]
    lane = lax.broadcasted_iota(jnp.int32, (EXTRA, kw), 1)
    line = lax.broadcasted_iota(jnp.int32, (EXTRA, kw), 0)
    sums = jnp.zeros((EXTRA, kw), F32)
    own = jnp.zeros((EXTRA, kw), F32)
    for i, term in enumerate(terms):
        sums = jnp.where(lane == i, term, sums)
        own = jnp.where(lane == OWN + i, term, own)
    for i in range(4):
        sums = jnp.where(lane == 3 + i, pairs[i].astype(F32), sums)
    out[tokens : tokens + EXTRA, :] = jnp.where(line == 0, sums, 0.0).astype(BF)
    mark[...] = jnp.where(line == 0, own, 0.0).astype(BF)


def prepared(place, limits, pairs, weights, gains, keys, ratios):
    tokens, kw = keys.shape
    scalar = pl.BlockSpec(memory_space=pltpu.SMEM)
    whole = pl.BlockSpec(memory_space=pltpu.VMEM)
    return pl.pallas_call(
        prepare_kernel,
        in_specs=[scalar] * 3 + [whole] * 4,
        out_specs=[whole] * 2,
        out_shape=[
            jax.ShapeDtypeStruct((2 * tokens + EXTRA, kw), BF),
            jax.ShapeDtypeStruct((EXTRA, kw), BF),
        ],
    )(place, limits, pairs, weights, gains, keys, ratios)


def join_kernel(payload, mark, out):
    rows = out.shape[0]
    out[: rows - EXTRA, :] = payload[: rows - EXTRA, :]
    out[rows - EXTRA :, :] = payload[rows - EXTRA : rows, :] + mark[...]


def joined(payload, mark):
    rows, kw = (payload.shape[0] + EXTRA) // 2, payload.shape[1]
    whole = pl.BlockSpec(memory_space=pltpu.VMEM)
    return pl.pallas_call(
        join_kernel,
        in_specs=[whole] * 2,
        out_specs=whole,
        out_shape=jax.ShapeDtypeStruct((rows, kw), BF),
        cost_estimate=FREE,
    )(payload, mark)


def coefficients(ratios, pairs):
    signs = [1.0, 1.0, -1.0, -1.0]
    out = []
    for row in range(4):
        margin = jnp.zeros_like(ratios[0])
        for other in range(4):
            margin += jnp.where(pairs[other] == pairs[row], signs[other] * ratios[other], 0.0)
        out.append(-DPO_BETA * signs[row] / (1.0 + jnp.exp(DPO_BETA * margin)))
    return out


def coef_kernel(place, pairs, gathered, out, notes, sem):
    copy = pltpu.make_async_copy(
        gathered.at[:, pl.ds(gathered.shape[1] - EXTRA, EXTRA), pl.ds(0, 128)], notes, sem
    )
    copy.start()
    copy.wait()
    row = place[2]
    values = jnp.sum(notes[...].astype(F32).reshape(4, -1, EXTRA, notes.shape[2]), axis=1)

    def ratios(first):
        picked = values[:, :1, first : first + 3]
        return [jnp.sum(picked[r], axis=1, keepdims=True) for r in range(4)]

    first = notes[0, :1, :16].astype(F32)
    own = coefficients(ratios(OWN), [pairs[i].astype(F32) for i in range(4)])
    following = coefficients(ratios(0), [first[:, 3 + i : 4 + i] for i in range(4)])
    lane = lax.broadcasted_iota(jnp.int32, out.shape, 1)
    result = jnp.zeros(out.shape, F32)
    for r in range(4):
        result = jnp.where(lane == lax.rem(row - r + 4, 4), own[r], result)
        result = jnp.where((lane == 4) & (row == r), following[r], result)
    out[...] = result


def coef_table(place, pairs, gathered):
    scalar = pl.BlockSpec(memory_space=pltpu.SMEM)
    return pl.pallas_call(
        coef_kernel,
        in_specs=[scalar, scalar, ANYWHERE],
        out_specs=pl.BlockSpec(memory_space=pltpu.VMEM),
        out_shape=jax.ShapeDtypeStruct((8, 128), F32),
        scratch_shapes=[
            pltpu.VMEM((gathered.shape[0], EXTRA, 128), BF),
            pltpu.SemaphoreType.DMA,
        ],
        cost_estimate=FREE,
    )(place, pairs, gathered)


def finish_kernel(coefs, first, second, third, fourth, gains, weights, out, sums):
    total = first[...] * coefs[:1, :1]
    for i, wave in enumerate((second, third, fourth)):
        total += wave[...].astype(F32) * coefs[:1, i + 1 : i + 2]
    out[...] = (total * as_column(gains[...])).astype(BF)
    found = jnp.sum(total * weights[...].astype(F32), axis=1, keepdims=True)
    sums[...] = jnp.broadcast_to(found, (found.shape[0], 128)).T[:1].astype(BF)


def finished(coefs, waves, gains, weights):
    whole = pl.BlockSpec(memory_space=pltpu.VMEM)
    rows, kw = weights.shape
    return pl.pallas_call(
        finish_kernel,
        in_specs=[whole] * 7,
        out_specs=[whole] * 2,
        out_shape=[jax.ShapeDtypeStruct((rows, kw), BF), jax.ShapeDtypeStruct((1, rows), BF)],
        cost_estimate=FREE,
    )(coefs, *waves, gains, weights)


ORDER = (2, 1, 3, 0)


def block_products(spot, other, hidden, keys, terms, out, sem):
    y, z = spot[1], spot[2]
    core = 1 - spot[0] if other else spot[0]
    for r in ORDER:

        def block(q, carry):
            at = lax.rem(z + q, 4) * 8 + lax.rem(y + r, 4) * 2 + core
            columns = hidden[:, pl.ds(pl.multiple_of(at * BLK, BLK), BLK)]
            terms[r, q] = lax.dot_general(
                columns, keys[...], (((0,), (0,)), ((), ())), preferred_element_type=F32
            ).astype(BF)
            return carry

        lax.fori_loop(0, 4, block, 0)
        pltpu.make_async_copy(terms.at[r], out.at[r], sem.at[r]).start()
    for r in ORDER:
        pltpu.make_async_copy(terms.at[r], out.at[r], sem.at[r]).wait()


def load(source, target, sem, parts):
    rows = source.shape[0] // parts
    copies = []
    for i in range(parts):
        at = pl.ds(i * rows, rows)
        copies.append(pltpu.make_async_copy(source.at[at], target.at[at], sem.at[i]))
        copies[-1].start()
    return copies


def send_kernel(spot, payload, hidden, *refs):
    out, *quarters, keys, states, terms, in_sem, out_sem, row_sem = refs
    parts = 4
    rows = states.shape[0] // parts
    for i, copy in enumerate(load(hidden, states, in_sem, parts)):
        copy.wait()

        def line(j, carry):
            at = pl.ds(pl.multiple_of(i * rows + j * 16, 16), 16)
            square = jnp.zeros((16, 512), F32)
            for c in range(0, states.shape[1], 512):
                part = states[at, c : c + 512].astype(F32)
                square = square + part * part
            inv = lax.rsqrt(jnp.sum(square, axis=1, keepdims=True) / states.shape[1] + EPS)
            from_key = pl.ds(pl.multiple_of(states.shape[0] + EXTRA + i * rows + j * 16, 16), 16)
            keys[at, :] = (payload[from_key, :].astype(F32) * inv).astype(BF)
            return carry

        lax.fori_loop(0, rows // 16, line, 0)
    copies = [
        pltpu.make_async_copy(states.at[pl.ds(i * QUARTER, QUARTER)], quarter, row_sem.at[i])
        for i, quarter in enumerate(quarters)
    ]
    for copy in copies:
        copy.start()
    block_products(spot, True, states, keys, terms, out, out_sem)
    for copy in copies:
        copy.wait()


def keep_kernel(spot, keys, hidden, *refs):
    out, states, terms, in_sem, out_sem, _ = refs
    for copy in load(hidden, states, in_sem, 4):
        copy.wait()
    block_products(spot, False, states, keys, terms, out, out_sem)


def term_call(kernel, operands, sending):
    tokens, width = operands[2].shape
    kw = operands[1].shape[1]
    whole = pl.BlockSpec(memory_space=pltpu.VMEM)
    more = [jax.ShapeDtypeStruct((QUARTER, width), BF)] * 4 if sending else []
    keys = [jax.ShapeDtypeStruct((tokens, kw), BF)] if sending else []
    return pl.pallas_call(
        kernel,
        in_specs=[pl.BlockSpec(memory_space=pltpu.SMEM), whole, ANYWHERE],
        out_specs=[ANYWHERE] * (1 + len(more)) + [whole] * len(keys),
        out_shape=[jax.ShapeDtypeStruct((4, 4, BLK, kw), BF), *more, *keys],
        scratch_shapes=[
            pltpu.VMEM((tokens, width), BF),
            pltpu.VMEM((4, 4, BLK, kw), BF),
            pltpu.SemaphoreType.DMA((4,)),
            pltpu.SemaphoreType.DMA((4,)),
            pltpu.SemaphoreType.DMA((4,)),
        ],
        compiler_params=pltpu.CompilerParams(vmem_limit_bytes=VMEM_LIMIT),
        cost_estimate=FREE,
    )(*operands)


def around(value, steps):
    return moved(value, lambda z_hi, x, z_lo, y, core: (z_hi, x, z_lo, (y + steps) % 4, core))


def along(value, steps):
    return moved(value, lambda z_hi, x, z_lo, y, core: (z_hi, x, (z_lo + steps) % 4, y, core))


def added(*parts):
    return sum(part.astype(F32) for part in parts)


def grad_kernel(payload, weights, out, held, slopes, in_sem, out_sem):
    tokens, parts = out.shape[0], in_sem.shape[0]
    count, rows, kw = held.shape
    step = count // parts
    keys = payload[payload.shape[0] - tokens :, :]
    copies = []
    for i in range(parts):
        at = pl.ds(i * step, step)
        copies.append(
            pltpu.make_async_copy(weights.at[at, pl.ds(0, rows)], held.at[at], in_sem.at[i])
        )
        copies[-1].start()
    for i in range(parts):
        copies[i].wait()
        block = held[i * step : (i + 1) * step].reshape(step * rows, kw)
        span = pl.ds(i * step * rows, step * rows)
        slopes[:, span] = lax.dot_general(
            keys, block, (((1,), (1,)), ((), ())), preferred_element_type=F32
        ).astype(BF)
        copies[i] = pltpu.make_async_copy(slopes.at[:, span], out.at[:, span], out_sem.at[i])
        copies[i].start()
    for copy in copies:
        copy.wait()


def unit_grads(payload, gathered, tokens):
    count, _, kw = gathered.shape
    parts = 4
    return pl.pallas_call(
        grad_kernel,
        in_specs=[pl.BlockSpec(memory_space=pltpu.VMEM), ANYWHERE],
        out_specs=ANYWHERE,
        out_shape=jax.ShapeDtypeStruct((tokens, count * BLK), BF),
        scratch_shapes=[
            pltpu.VMEM((count, BLK, kw), BF),
            pltpu.VMEM((tokens, count * BLK), BF),
            pltpu.SemaphoreType.DMA((parts,)),
            pltpu.SemaphoreType.DMA((parts,)),
        ],
        compiler_params=pltpu.CompilerParams(vmem_limit_bytes=VMEM_LIMIT),
        cost_estimate=FREE,
    )(payload, gathered)


def section_kernel(near_rows, far_rows, scale, is_far, slopes, *refs):
    count = len(near_rows)
    near, far = refs[:count], refs[count : count + len(far_rows)]
    out, rows, grads, done, row_sem, grad_sem, out_sem = refs[count + len(far_rows) :]
    tokens, width = rows.shape
    group, span = 16, 512
    parts = tokens // PIECE

    def fetched(sources, sizes):
        first = 0
        for source, size in zip(sources, sizes):
            for at in range(0, size, PIECE):
                spot = (first + at) // PIECE
                pltpu.make_async_copy(
                    source.at[pl.ds(at, PIECE)], rows.at[pl.ds(first + at, PIECE)], row_sem.at[spot]
                ).start()
            first += size

    def whole(i):
        return pl.ds(pl.multiple_of(i * PIECE, PIECE), PIECE)

    for i in range(parts):
        at = pl.ds(i * PIECE, PIECE)
        pltpu.make_async_copy(slopes.at[at], grads.at[at], grad_sem.at[i]).start()

    @pl.when(is_far[0] == 1)
    def _():
        fetched(far, far_rows)

    @pl.when(is_far[0] != 1)
    def _():
        fetched(near, near_rows)

    factor = scale[:1, 4:5]

    def part(i, carry):
        at = whole(i)
        pltpu.make_async_copy(slopes.at[at], grads.at[at], grad_sem.at[i]).wait()
        pltpu.make_async_copy(slopes.at[at], rows.at[at], row_sem.at[i]).wait()
        for g in range(PIECE // group):
            line = pl.ds(pl.multiple_of(i * PIECE + g * group, group), group)
            square = jnp.zeros((group, span), F32)
            cross = jnp.zeros((group, span), F32)
            for c in range(0, width, span):
                h = rows[line, c : c + span].astype(F32)
                square = square + h * h
                cross = cross + h * grads[line, c : c + span].astype(F32)
            inv = lax.rsqrt(jnp.sum(square, axis=1, keepdims=True) / width + EPS)
            inner = jnp.sum(cross, axis=1, keepdims=True) / width * inv * factor
            ahead, back = inv * factor, inv * inv * inner
            for c in range(0, width, span):
                h = rows[line, c : c + span].astype(F32)
                u = grads[line, c : c + span].astype(F32)
                done[line, c : c + span] = (ahead * u - back * h).astype(BF)
        pltpu.make_async_copy(done.at[at], out.at[at], out_sem.at[i]).start()
        return carry

    lax.fori_loop(0, parts, part, 0)
    for i in range(parts):
        at = pl.ds(i * PIECE, PIECE)
        pltpu.make_async_copy(done.at[at], out.at[at], out_sem.at[i]).wait()


def section_grads(scale, is_far, slopes, near, far):
    tokens, width = slopes.shape
    scalar = pl.BlockSpec(memory_space=pltpu.SMEM)
    near_rows, far_rows = [v.shape[0] for v in near], [v.shape[0] for v in far]
    parts = tokens // PIECE
    return pl.pallas_call(
        functools.partial(section_kernel, near_rows, far_rows),
        in_specs=[pl.BlockSpec(memory_space=pltpu.VMEM), scalar] + [ANYWHERE] * (1 + len(near) + len(far)),
        out_specs=ANYWHERE,
        out_shape=jax.ShapeDtypeStruct((tokens, width), BF),
        scratch_shapes=[pltpu.VMEM((tokens, width), BF)] * 3
        + [pltpu.SemaphoreType.DMA((parts,))] * 3,
        compiler_params=pltpu.CompilerParams(vmem_limit_bytes=VMEM_LIMIT),
        cost_estimate=FREE,
    )(scale, is_far, slopes, *near, *far)


def on_device(hidden, norm_gain, key_weight, key_cotangent, token_logratio, lengths, pair_of_row):
    states = hidden[0]
    weights = key_weight[0]
    tokens, width = states.shape
    kw = weights.shape[1]
    section, dp = lax.axis_index("section"), lax.axis_index("dp")
    core, y, z = dp % 2, (dp // 2) % 4, dp // 8
    place = jnp.stack([core, y, z, (dp * tokens) % ROW_LEN]).astype(jnp.int32)

    payload, mark = prepared(
        place, lengths[0], pair_of_row[0], weights, norm_gain, key_cotangent[0], token_logratio
    )
    following = to_previous(payload)

    send, *quarters, keys = term_call(send_kernel, (place, payload, states), True)
    following = gated([following], [keys])[0]
    joint = joined(following, mark)
    send = gated([send], [joint])[0]
    gathered = lax.all_gather(joint, "dp", axis=0, tiled=True)
    gathered = gathered.reshape(-1, tokens + EXTRA, kw)
    near = lowered(states)
    up = (1, 0)
    direct = stepped(quarters[0], up, (0, 3))
    spread = {x: stepped(quarters[x], up, (1, x)) for x in (2, 3, 1)}

    def over_cores(operands):
        states, keys, place, send = operands
        swapped = moved(send, lambda z_hi, x, z_lo, y, core: (z_hi, x, z_lo, y, 1 - core))
        return swapped, *term_call(keep_kernel, (place, keys, states), False)

    def over_far_chips(operands):
        swapped, keep = operands
        sums = lambda r, *more: added(keep[r], swapped[r], *more)
        far = sums(2).astype(BF)
        far_up, far_down = around(far[:2], 1), around(far[2:], -1)
        up_terms = jnp.concatenate([far_up.astype(F32), jnp.zeros(far_up.shape, F32)])
        down_terms = jnp.concatenate([jnp.zeros(far_down.shape, F32), far_down.astype(F32)])
        return sums(0).astype(BF), sums(1, up_terms).astype(BF), sums(3, down_terms).astype(BF)

    def over_chips(operands):
        here, up_terms, down_terms = operands
        plane = added(here, around(up_terms, 1), around(down_terms, -1))
        return plane[0], *[plane[i].astype(BF) for i in (1, 2, 3)]

    def staged(step, operands):
        shapes = jax.eval_shape(step, operands)
        blank = lambda _: jax.tree.map(lambda v: jnp.zeros(v.shape, v.dtype), shapes)
        return lax.cond(dp < tokens, step, blank, operands)

    sums = staged(over_cores, (states, keys, place, send))
    second, third, first = gated([spread[x] for x in (2, 3, 1)], sums[:1])
    crossing = picked(section, [first, second, third])
    crossed = moved(
        crossing, lambda z_hi, x, z_lo, y, core: (0, x, z_lo, y, core) if z_hi and x else None
    )
    plane = staged(over_chips, staged(over_far_chips, sums))
    crossed = gated([crossed], plane[:1])[0]
    far = [direct, *[stepped(crossed, (0, x), (0, 3)) for x in (1, 2)], crossed]
    slopes = unit_grads(following, gathered, tokens)
    coefs = coef_table(place, pair_of_row[0], gathered)
    later = gated(plane[1:], [near])
    waves = [plane[0], *[along(wave, i + 1) for i, wave in enumerate(later)]]
    weight_grad, gain_grad = finished(coefs, waves, norm_gain, weights)

    is_far = (section == 3).astype(jnp.int32)[None]
    out = section_grads(coefs, is_far, slopes, [near], far)
    return out[None], weight_grad[None], gain_grad


def solution(mesh):
    in_specs = (
        P("section", "dp", None),
        P("section", "dp"),
        P("section", "dp", None),
        P("section", "dp", None),
        P("section", "dp"),
        P("section", None),
        P("section", None),
    )
    out_specs = (P("section", "dp", None), P("section", "dp", None), P("section", "dp"))
    return jax.shard_map(
        on_device, mesh=mesh, in_specs=in_specs, out_specs=out_specs, check_vma=False
    )
```

```python
import functools
import jax
import jax.numpy as jnp
from jax import lax
from jax.experimental import pallas as pl
from jax.experimental.pallas import tpu as pltpu
from jax.sharding import PartitionSpec as P

ROW_LEN = 2048
DPO_BETA = 0.1
EPS = 1e-06
AXES = ("section", "dp")
BF, F32 = jnp.bfloat16, jnp.float32
BLK = 256
PIECE = 64
FREE = pl.CostEstimate(flops=0, bytes_accessed=0, transcendentals=0)
EXTRA = 16
QUARTER = 64
OWN = 16
VMEM_LIMIT = 56 * 1024 * 1024


def index_of(z_hi, x, z_lo, y, core):
    return ((z_hi * 4 + x) * 4 + z_lo) * 8 + y * 2 + core


def moved(value, target):
    pairs = []
    for z_hi in range(2):
        for x in range(4):
            for z_lo in range(4):
                for y in range(4):
                    for core in range(2):
                        goal = target(z_hi, x, z_lo, y, core)
                        if goal is not None:
                            pairs.append((index_of(z_hi, x, z_lo, y, core), index_of(*goal)))
    return lax.ppermute(value, AXES, pairs)


def to_previous(value):
    def target(z_hi, x, z_lo, y, core):
        section = z_hi * 4 + x - 1
        return None if section < 0 else (section // 4, section % 4, z_lo, y, core)

    return moved(value, target)


ANYWHERE = pl.BlockSpec(memory_space=pl.ANY)


def gated(values, events):
    count = len(values)
    return pl.pallas_call(
        lambda *refs: None,
        in_specs=[ANYWHERE] * (count + len(events)),
        out_specs=[ANYWHERE] * count,
        out_shape=[jax.ShapeDtypeStruct(v.shape, v.dtype) for v in values],
        input_output_aliases={i: i for i in range(count)},
        cost_estimate=FREE,
    )(*values, *events)


def stepped(value, source, goal):
    return moved(
        value,
        lambda z_hi, x, z_lo, y, core: (*goal, z_lo, y, core) if (z_hi, x) == source else None,
    )


def lowered(value):
    return moved(
        value, lambda z_hi, x, z_lo, y, core: (z_hi, x - 1, z_lo, y, core) if x else None
    )


def picked_kernel(section, *refs):
    *sources, out, held, sem = refs
    for i, source in enumerate(sources):

        @pl.when(section[0] == 5 + i)
        def _():
            for start, end in ((source, held), (held, out)):
                copy = pltpu.make_async_copy(start, end, sem)
                copy.start()
                copy.wait()


def picked(section, sources):
    shape = sources[0].shape
    return pl.pallas_call(
        picked_kernel,
        in_specs=[pl.BlockSpec(memory_space=pltpu.SMEM)] + [ANYWHERE] * 3,
        out_specs=ANYWHERE,
        out_shape=jax.ShapeDtypeStruct(shape, BF),
        scratch_shapes=[pltpu.VMEM(shape, BF), pltpu.SemaphoreType.DMA],
        compiler_params=pltpu.CompilerParams(vmem_limit_bytes=VMEM_LIMIT),
        cost_estimate=FREE,
    )(section[None], *sources)


def as_column(row):
    return jnp.broadcast_to(row.astype(F32), (128, row.shape[1])).T[:, :1]


def prepare_kernel(place, limits, pairs, weights, gains, keys, ratios, out, mark):
    tokens, kw = keys.shape
    out[:tokens, :] = (weights[...].astype(F32) * as_column(gains[...])).astype(BF)
    limit = limits[place[2]] - place[3]
    valid = lax.broadcasted_iota(jnp.int32, (tokens, kw), 0) < limit
    out[tokens + EXTRA :, :] = jnp.where(valid, keys[...], jnp.zeros_like(keys))
    kept = lax.broadcasted_iota(jnp.int32, ratios.shape, 1) < limit
    partial = jnp.sum(jnp.where(kept, ratios[...], 0.0), axis=1, keepdims=True)
    high = partial.astype(BF).astype(F32)
    middle = (partial - high).astype(BF).astype(F32)
    terms = [high, middle, partial - high - middle]
    lane = lax.broadcasted_iota(jnp.int32, (EXTRA, kw), 1)
    line = lax.broadcasted_iota(jnp.int32, (EXTRA, kw), 0)
    sums = jnp.zeros((EXTRA, kw), F32)
    own = jnp.zeros((EXTRA, kw), F32)
    for i, term in enumerate(terms):
        sums = jnp.where(lane == i, term, sums)
        own = jnp.where(lane == OWN + i, term, own)
    for i in range(4):
        sums = jnp.where(lane == 3 + i, pairs[i].astype(F32), sums)
    out[tokens : tokens + EXTRA, :] = jnp.where(line == 0, sums, 0.0).astype(BF)
    mark[...] = jnp.where(line == 0, own, 0.0).astype(BF)


def prepared(place, limits, pairs, weights, gains, keys, ratios):
    tokens, kw = keys.shape
    scalar = pl.BlockSpec(memory_space=pltpu.SMEM)
    whole = pl.BlockSpec(memory_space=pltpu.VMEM)
    return pl.pallas_call(
        prepare_kernel,
        in_specs=[scalar] * 3 + [whole] * 4,
        out_specs=[whole] * 2,
        out_shape=[
            jax.ShapeDtypeStruct((2 * tokens + EXTRA, kw), BF),
            jax.ShapeDtypeStruct((EXTRA, kw), BF),
        ],
    )(place, limits, pairs, weights, gains, keys, ratios)


def join_kernel(payload, mark, out):
    rows = out.shape[0]
    out[: rows - EXTRA, :] = payload[: rows - EXTRA, :]
    out[rows - EXTRA :, :] = payload[rows - EXTRA : rows, :] + mark[...]


def joined(payload, mark):
    rows, kw = (payload.shape[0] + EXTRA) // 2, payload.shape[1]
    whole = pl.BlockSpec(memory_space=pltpu.VMEM)
    return pl.pallas_call(
        join_kernel,
        in_specs=[whole] * 2,
        out_specs=whole,
        out_shape=jax.ShapeDtypeStruct((rows, kw), BF),
        cost_estimate=FREE,
    )(payload, mark)


def coefficients(ratios, pairs):
    signs = [1.0, 1.0, -1.0, -1.0]
    out = []
    for row in range(4):
        margin = jnp.zeros_like(ratios[0])
        for other in range(4):
            margin += jnp.where(pairs[other] == pairs[row], signs[other] * ratios[other], 0.0)
        out.append(-DPO_BETA * signs[row] / (1.0 + jnp.exp(DPO_BETA * margin)))
    return out


def coef_kernel(place, pairs, gathered, out, notes, sem):
    copy = pltpu.make_async_copy(
        gathered.at[:, pl.ds(gathered.shape[1] - EXTRA, EXTRA), pl.ds(0, 128)], notes, sem
    )
    copy.start()
    copy.wait()
    row = place[2]
    values = jnp.sum(notes[...].astype(F32).reshape(4, -1, EXTRA, notes.shape[2]), axis=1)

    def ratios(first):
        picked = values[:, :1, first : first + 3]
        return [jnp.sum(picked[r], axis=1, keepdims=True) for r in range(4)]

    first = notes[0, :1, :16].astype(F32)
    own = coefficients(ratios(OWN), [pairs[i].astype(F32) for i in range(4)])
    following = coefficients(ratios(0), [first[:, 3 + i : 4 + i] for i in range(4)])
    lane = lax.broadcasted_iota(jnp.int32, out.shape, 1)
    result = jnp.zeros(out.shape, F32)
    for r in range(4):
        result = jnp.where(lane == lax.rem(row - r + 4, 4), own[r], result)
        result = jnp.where((lane == 4) & (row == r), following[r], result)
    out[...] = result


def coef_table(place, pairs, gathered):
    scalar = pl.BlockSpec(memory_space=pltpu.SMEM)
    return pl.pallas_call(
        coef_kernel,
        in_specs=[scalar, scalar, ANYWHERE],
        out_specs=pl.BlockSpec(memory_space=pltpu.VMEM),
        out_shape=jax.ShapeDtypeStruct((8, 128), F32),
        scratch_shapes=[
            pltpu.VMEM((gathered.shape[0], EXTRA, 128), BF),
            pltpu.SemaphoreType.DMA,
        ],
        cost_estimate=FREE,
    )(place, pairs, gathered)


def finish_kernel(coefs, first, second, third, fourth, gains, weights, out, sums):
    total = first[...] * coefs[:1, :1]
    for i, wave in enumerate((second, third, fourth)):
        total += wave[...].astype(F32) * coefs[:1, i + 1 : i + 2]
    out[...] = (total * as_column(gains[...])).astype(BF)
    found = jnp.sum(total * weights[...].astype(F32), axis=1, keepdims=True)
    sums[...] = jnp.broadcast_to(found, (found.shape[0], 128)).T[:1].astype(BF)


def finished(coefs, waves, gains, weights):
    whole = pl.BlockSpec(memory_space=pltpu.VMEM)
    rows, kw = weights.shape
    return pl.pallas_call(
        finish_kernel,
        in_specs=[whole] * 7,
        out_specs=[whole] * 2,
        out_shape=[jax.ShapeDtypeStruct((rows, kw), BF), jax.ShapeDtypeStruct((1, rows), BF)],
        cost_estimate=FREE,
    )(coefs, *waves, gains, weights)


ORDER = (2, 1, 3, 0)


def block_products(spot, other, hidden, keys, terms, out, sem):
    y, z = spot[1], spot[2]
    core = 1 - spot[0] if other else spot[0]
    for r in ORDER:

        def block(q, carry):
            at = lax.rem(z + q, 4) * 8 + lax.rem(y + r, 4) * 2 + core
            columns = hidden[:, pl.ds(pl.multiple_of(at * BLK, BLK), BLK)]
            terms[r, q] = lax.dot_general(
                columns, keys[...], (((0,), (0,)), ((), ())), preferred_element_type=F32
            ).astype(BF)
            return carry

        lax.fori_loop(0, 4, block, 0)
        pltpu.make_async_copy(terms.at[r], out.at[r], sem.at[r]).start()
    for r in ORDER:
        pltpu.make_async_copy(terms.at[r], out.at[r], sem.at[r]).wait()


def load(source, target, sem, parts):
    rows = source.shape[0] // parts
    copies = []
    for i in range(parts):
        at = pl.ds(i * rows, rows)
        copies.append(pltpu.make_async_copy(source.at[at], target.at[at], sem.at[i]))
        copies[-1].start()
    return copies


def send_kernel(spot, payload, hidden, *refs):
    out, *quarters, keys, states, terms, in_sem, out_sem, row_sem = refs
    parts = 4
    rows = states.shape[0] // parts
    for i, copy in enumerate(load(hidden, states, in_sem, parts)):
        copy.wait()

        def line(j, carry):
            at = pl.ds(pl.multiple_of(i * rows + j * 16, 16), 16)
            square = jnp.zeros((16, 512), F32)
            for c in range(0, states.shape[1], 512):
                part = states[at, c : c + 512].astype(F32)
                square = square + part * part
            inv = lax.rsqrt(jnp.sum(square, axis=1, keepdims=True) / states.shape[1] + EPS)
            from_key = pl.ds(pl.multiple_of(states.shape[0] + EXTRA + i * rows + j * 16, 16), 16)
            keys[at, :] = (payload[from_key, :].astype(F32) * inv).astype(BF)
            return carry

        lax.fori_loop(0, rows // 16, line, 0)
    copies = [
        pltpu.make_async_copy(states.at[pl.ds(i * QUARTER, QUARTER)], quarter, row_sem.at[i])
        for i, quarter in enumerate(quarters)
    ]
    for copy in copies:
        copy.start()
    block_products(spot, True, states, keys, terms, out, out_sem)
    for copy in copies:
        copy.wait()


def keep_kernel(spot, keys, hidden, *refs):
    out, states, terms, in_sem, out_sem, _ = refs
    for copy in load(hidden, states, in_sem, 4):
        copy.wait()
    block_products(spot, False, states, keys, terms, out, out_sem)


def term_call(kernel, operands, sending):
    tokens, width = operands[2].shape
    kw = operands[1].shape[1]
    whole = pl.BlockSpec(memory_space=pltpu.VMEM)
    more = [jax.ShapeDtypeStruct((QUARTER, width), BF)] * 4 if sending else []
    keys = [jax.ShapeDtypeStruct((tokens, kw), BF)] if sending else []
    return pl.pallas_call(
        kernel,
        in_specs=[pl.BlockSpec(memory_space=pltpu.SMEM), whole, ANYWHERE],
        out_specs=[ANYWHERE] * (1 + len(more)) + [whole] * len(keys),
        out_shape=[jax.ShapeDtypeStruct((4, 4, BLK, kw), BF), *more, *keys],
        scratch_shapes=[
            pltpu.VMEM((tokens, width), BF),
            pltpu.VMEM((4, 4, BLK, kw), BF),
            pltpu.SemaphoreType.DMA((4,)),
            pltpu.SemaphoreType.DMA((4,)),
            pltpu.SemaphoreType.DMA((4,)),
        ],
        compiler_params=pltpu.CompilerParams(vmem_limit_bytes=VMEM_LIMIT),
        cost_estimate=FREE,
    )(*operands)


def around(value, steps):
    return moved(value, lambda z_hi, x, z_lo, y, core: (z_hi, x, z_lo, (y + steps) % 4, core))


def along(value, steps):
    return moved(value, lambda z_hi, x, z_lo, y, core: (z_hi, x, (z_lo + steps) % 4, y, core))


def added(*parts):
    return sum(part.astype(F32) for part in parts)


def grad_kernel(payload, weights, out, held, slopes, in_sem, out_sem):
    tokens, parts = out.shape[0], in_sem.shape[0]
    count, rows, kw = held.shape
    step = count // parts
    keys = payload[payload.shape[0] - tokens :, :]
    copies = []
    for i in range(parts):
        at = pl.ds(i * step, step)
        copies.append(
            pltpu.make_async_copy(weights.at[at, pl.ds(0, rows)], held.at[at], in_sem.at[i])
        )
        copies[-1].start()
    for i in range(parts):
        copies[i].wait()
        block = held[i * step : (i + 1) * step].reshape(step * rows, kw)
        span = pl.ds(i * step * rows, step * rows)
        slopes[:, span] = lax.dot_general(
            keys, block, (((1,), (1,)), ((), ())), preferred_element_type=F32
        ).astype(BF)
        copies[i] = pltpu.make_async_copy(slopes.at[:, span], out.at[:, span], out_sem.at[i])
        copies[i].start()
    for copy in copies:
        copy.wait()


def unit_grads(payload, gathered, tokens):
    count, _, kw = gathered.shape
    parts = 4
    return pl.pallas_call(
        grad_kernel,
        in_specs=[pl.BlockSpec(memory_space=pltpu.VMEM), ANYWHERE],
        out_specs=ANYWHERE,
        out_shape=jax.ShapeDtypeStruct((tokens, count * BLK), BF),
        scratch_shapes=[
            pltpu.VMEM((count, BLK, kw), BF),
            pltpu.VMEM((tokens, count * BLK), BF),
            pltpu.SemaphoreType.DMA((parts,)),
            pltpu.SemaphoreType.DMA((parts,)),
        ],
        compiler_params=pltpu.CompilerParams(vmem_limit_bytes=VMEM_LIMIT),
        cost_estimate=FREE,
    )(payload, gathered)


def section_kernel(near_rows, far_rows, scale, is_far, slopes, *refs):
    count = len(near_rows)
    near, far = refs[:count], refs[count : count + len(far_rows)]
    out, rows, grads, done, row_sem, grad_sem, out_sem = refs[count + len(far_rows) :]
    tokens, width = rows.shape
    group, span = 16, 512
    parts = tokens // PIECE

    def fetched(sources, sizes):
        first = 0
        for source, size in zip(sources, sizes):
            for at in range(0, size, PIECE):
                spot = (first + at) // PIECE
                pltpu.make_async_copy(
                    source.at[pl.ds(at, PIECE)], rows.at[pl.ds(first + at, PIECE)], row_sem.at[spot]
                ).start()
            first += size

    def whole(i):
        return pl.ds(pl.multiple_of(i * PIECE, PIECE), PIECE)

    for i in range(parts):
        at = pl.ds(i * PIECE, PIECE)
        pltpu.make_async_copy(slopes.at[at], grads.at[at], grad_sem.at[i]).start()

    @pl.when(is_far[0] == 1)
    def _():
        fetched(far, far_rows)

    @pl.when(is_far[0] != 1)
    def _():
        fetched(near, near_rows)

    factor = scale[:1, 4:5]

    def part(i, carry):
        at = whole(i)
        pltpu.make_async_copy(slopes.at[at], grads.at[at], grad_sem.at[i]).wait()
        pltpu.make_async_copy(slopes.at[at], rows.at[at], row_sem.at[i]).wait()
        for g in range(PIECE // group):
            line = pl.ds(pl.multiple_of(i * PIECE + g * group, group), group)
            square = jnp.zeros((group, span), F32)
            cross = jnp.zeros((group, span), F32)
            for c in range(0, width, span):
                h = rows[line, c : c + span].astype(F32)
                square = square + h * h
                cross = cross + h * grads[line, c : c + span].astype(F32)
            inv = lax.rsqrt(jnp.sum(square, axis=1, keepdims=True) / width + EPS)
            inner = jnp.sum(cross, axis=1, keepdims=True) / width * inv * factor
            ahead, back = inv * factor, inv * inv * inner
            for c in range(0, width, span):
                h = rows[line, c : c + span].astype(F32)
                u = grads[line, c : c + span].astype(F32)
                done[line, c : c + span] = (ahead * u - back * h).astype(BF)
        pltpu.make_async_copy(done.at[at], out.at[at], out_sem.at[i]).start()
        return carry

    lax.fori_loop(0, parts, part, 0)
    for i in range(parts):
        at = pl.ds(i * PIECE, PIECE)
        pltpu.make_async_copy(done.at[at], out.at[at], out_sem.at[i]).wait()


def section_grads(scale, is_far, slopes, near, far):
    tokens, width = slopes.shape
    scalar = pl.BlockSpec(memory_space=pltpu.SMEM)
    near_rows, far_rows = [v.shape[0] for v in near], [v.shape[0] for v in far]
    parts = tokens // PIECE
    return pl.pallas_call(
        functools.partial(section_kernel, near_rows, far_rows),
        in_specs=[pl.BlockSpec(memory_space=pltpu.VMEM), scalar] + [ANYWHERE] * (1 + len(near) + len(far)),
        out_specs=ANYWHERE,
        out_shape=jax.ShapeDtypeStruct((tokens, width), BF),
        scratch_shapes=[pltpu.VMEM((tokens, width), BF)] * 3
        + [pltpu.SemaphoreType.DMA((parts,))] * 3,
        compiler_params=pltpu.CompilerParams(vmem_limit_bytes=VMEM_LIMIT),
        cost_estimate=FREE,
    )(scale, is_far, slopes, *near, *far)


def on_device(hidden, norm_gain, key_weight, key_cotangent, token_logratio, lengths, pair_of_row):
    states = hidden[0]
    weights = key_weight[0]
    tokens, width = states.shape
    kw = weights.shape[1]
    section, dp = lax.axis_index("section"), lax.axis_index("dp")
    core, y, z = dp % 2, (dp // 2) % 4, dp // 8
    place = jnp.stack([core, y, z, (dp * tokens) % ROW_LEN]).astype(jnp.int32)

    payload, mark = prepared(
        place, lengths[0], pair_of_row[0], weights, norm_gain, key_cotangent[0], token_logratio
    )
    following = to_previous(payload)

    send, *quarters, keys = term_call(send_kernel, (place, payload, states), True)
    following = gated([following], [keys])[0]
    joint = joined(following, mark)
    send = gated([send], [joint])[0]
    gathered = lax.all_gather(joint, "dp", axis=0, tiled=True)
    gathered = gathered.reshape(-1, tokens + EXTRA, kw)
    near = lowered(states)
    up = (1, 0)
    direct = stepped(quarters[0], up, (0, 3))
    spread = {x: stepped(quarters[x], up, (1, x)) for x in (2, 3, 1)}

    def over_cores(operands):
        states, keys, place, send = operands
        swapped = moved(send, lambda z_hi, x, z_lo, y, core: (z_hi, x, z_lo, y, 1 - core))
        return swapped, *term_call(keep_kernel, (place, keys, states), False)

    def over_far_chips(operands):
        swapped, keep = operands
        sums = lambda r, *more: added(keep[r], swapped[r], *more)
        far = sums(2).astype(BF)
        far_up, far_down = around(far[:2], 1), around(far[2:], -1)
        up_terms = jnp.concatenate([far_up.astype(F32), jnp.zeros(far_up.shape, F32)])
        down_terms = jnp.concatenate([jnp.zeros(far_down.shape, F32), far_down.astype(F32)])
        return sums(0).astype(BF), sums(1, up_terms).astype(BF), sums(3, down_terms).astype(BF)

    def over_chips(operands):
        here, up_terms, down_terms = operands
        plane = added(here, around(up_terms, 1), around(down_terms, -1))
        return plane[0], *[plane[i].astype(BF) for i in (1, 2, 3)]

    def staged(step, operands):
        shapes = jax.eval_shape(step, operands)
        blank = lambda _: jax.tree.map(lambda v: jnp.zeros(v.shape, v.dtype), shapes)
        return lax.cond(dp < tokens, step, blank, operands)

    sums = staged(over_cores, (states, keys, place, send))
    second, third, first = gated([spread[x] for x in (2, 3, 1)], sums[:1])
    crossing = picked(section, [first, second, third])
    crossed = moved(
        crossing, lambda z_hi, x, z_lo, y, core: (0, x, z_lo, y, core) if z_hi and x else None
    )
    plane = staged(over_chips, staged(over_far_chips, sums))
    crossed = gated([crossed], plane[:1])[0]
    far = [direct, *[stepped(crossed, (0, x), (0, 3)) for x in (1, 2)], crossed]
    slopes = unit_grads(following, gathered, tokens)
    coefs = coef_table(place, pair_of_row[0], gathered)
    later = gated(plane[1:], [near])
    slopes = gated([slopes], [coefs])[0]
    first, last = along(later[0], 1), along(later[2], 3)
    middle = along(gated([later[1]], [slopes])[0], 2)
    waves = [plane[0], first, middle, last]
    weight_grad, gain_grad = finished(coefs, waves, norm_gain, weights)

    is_far = (section == 3).astype(jnp.int32)[None]
    out = section_grads(coefs, is_far, slopes, [near], far)
    return out[None], weight_grad[None], gain_grad


def solution(mesh):
    in_specs = (
        P("section", "dp", None),
        P("section", "dp"),
        P("section", "dp", None),
        P("section", "dp", None),
        P("section", "dp"),
        P("section", None),
        P("section", None),
    )
    out_specs = (P("section", "dp", None), P("section", "dp", None), P("section", "dp"))
    return jax.shard_map(
        on_device, mesh=mesh, in_specs=in_specs, out_specs=out_specs, check_vma=False
    )
```

```python
import functools
import jax
import jax.numpy as jnp
from jax import lax
from jax.experimental import pallas as pl
from jax.experimental.pallas import tpu as pltpu
from jax.sharding import PartitionSpec as P

ROW_LEN = 2048
DPO_BETA = 0.1
EPS = 1e-06
AXES = ("section", "dp")
BF, F32 = jnp.bfloat16, jnp.float32
BLK = 256
PIECE = 64
FREE = pl.CostEstimate(flops=0, bytes_accessed=0, transcendentals=0)
EXTRA = 16
QUARTER = 64
OWN = 16
VMEM_LIMIT = 56 * 1024 * 1024


def index_of(z_hi, x, z_lo, y, core):
    return ((z_hi * 4 + x) * 4 + z_lo) * 8 + y * 2 + core


def moved(value, target):
    pairs = []
    for z_hi in range(2):
        for x in range(4):
            for z_lo in range(4):
                for y in range(4):
                    for core in range(2):
                        goal = target(z_hi, x, z_lo, y, core)
                        if goal is not None:
                            pairs.append((index_of(z_hi, x, z_lo, y, core), index_of(*goal)))
    return lax.ppermute(value, AXES, pairs)


def to_previous(value):
    def target(z_hi, x, z_lo, y, core):
        section = z_hi * 4 + x - 1
        return None if section < 0 else (section // 4, section % 4, z_lo, y, core)

    return moved(value, target)


ANYWHERE = pl.BlockSpec(memory_space=pl.ANY)


def gated(values, events):
    count = len(values)
    return pl.pallas_call(
        lambda *refs: None,
        in_specs=[ANYWHERE] * (count + len(events)),
        out_specs=[ANYWHERE] * count,
        out_shape=[jax.ShapeDtypeStruct(v.shape, v.dtype) for v in values],
        input_output_aliases={i: i for i in range(count)},
        cost_estimate=FREE,
    )(*values, *events)


def stepped(value, source, goal):
    return moved(
        value,
        lambda z_hi, x, z_lo, y, core: (*goal, z_lo, y, core) if (z_hi, x) == source else None,
    )


def lowered(value):
    return moved(
        value, lambda z_hi, x, z_lo, y, core: (z_hi, x - 1, z_lo, y, core) if x else None
    )


def picked_kernel(section, *refs):
    *sources, out, held, sem = refs
    for i, source in enumerate(sources):

        @pl.when(section[0] == 5 + i)
        def _():
            for start, end in ((source, held), (held, out)):
                copy = pltpu.make_async_copy(start, end, sem)
                copy.start()
                copy.wait()


def picked(section, sources):
    shape = sources[0].shape
    return pl.pallas_call(
        picked_kernel,
        in_specs=[pl.BlockSpec(memory_space=pltpu.SMEM)] + [ANYWHERE] * 3,
        out_specs=ANYWHERE,
        out_shape=jax.ShapeDtypeStruct(shape, BF),
        scratch_shapes=[pltpu.VMEM(shape, BF), pltpu.SemaphoreType.DMA],
        compiler_params=pltpu.CompilerParams(vmem_limit_bytes=VMEM_LIMIT),
        cost_estimate=FREE,
    )(section[None], *sources)


def as_column(row):
    return jnp.broadcast_to(row.astype(F32), (128, row.shape[1])).T[:, :1]


def prepare_kernel(place, limits, pairs, weights, gains, keys, ratios, out, mark):
    tokens, kw = keys.shape
    out[:tokens, :] = (weights[...].astype(F32) * as_column(gains[...])).astype(BF)
    limit = limits[place[2]] - place[3]
    valid = lax.broadcasted_iota(jnp.int32, (tokens, kw), 0) < limit
    out[tokens + EXTRA :, :] = jnp.where(valid, keys[...], jnp.zeros_like(keys))
    kept = lax.broadcasted_iota(jnp.int32, ratios.shape, 1) < limit
    partial = jnp.sum(jnp.where(kept, ratios[...], 0.0), axis=1, keepdims=True)
    high = partial.astype(BF).astype(F32)
    middle = (partial - high).astype(BF).astype(F32)
    terms = [high, middle, partial - high - middle]
    lane = lax.broadcasted_iota(jnp.int32, (EXTRA, kw), 1)
    line = lax.broadcasted_iota(jnp.int32, (EXTRA, kw), 0)
    sums = jnp.zeros((EXTRA, kw), F32)
    own = jnp.zeros((EXTRA, kw), F32)
    for i, term in enumerate(terms):
        sums = jnp.where(lane == i, term, sums)
        own = jnp.where(lane == OWN + i, term, own)
    for i in range(4):
        sums = jnp.where(lane == 3 + i, pairs[i].astype(F32), sums)
    out[tokens : tokens + EXTRA, :] = jnp.where(line == 0, sums, 0.0).astype(BF)
    mark[...] = jnp.where(line == 0, own, 0.0).astype(BF)


def prepared(place, limits, pairs, weights, gains, keys, ratios):
    tokens, kw = keys.shape
    scalar = pl.BlockSpec(memory_space=pltpu.SMEM)
    whole = pl.BlockSpec(memory_space=pltpu.VMEM)
    return pl.pallas_call(
        prepare_kernel,
        in_specs=[scalar] * 3 + [whole] * 4,
        out_specs=[whole] * 2,
        out_shape=[
            jax.ShapeDtypeStruct((2 * tokens + EXTRA, kw), BF),
            jax.ShapeDtypeStruct((EXTRA, kw), BF),
        ],
    )(place, limits, pairs, weights, gains, keys, ratios)


def join_kernel(payload, mark, out):
    rows = out.shape[0]
    out[: rows - EXTRA, :] = payload[: rows - EXTRA, :]
    out[rows - EXTRA :, :] = payload[rows - EXTRA : rows, :] + mark[...]


def joined(payload, mark):
    rows, kw = (payload.shape[0] + EXTRA) // 2, payload.shape[1]
    whole = pl.BlockSpec(memory_space=pltpu.VMEM)
    return pl.pallas_call(
        join_kernel,
        in_specs=[whole] * 2,
        out_specs=whole,
        out_shape=jax.ShapeDtypeStruct((rows, kw), BF),
        cost_estimate=FREE,
    )(payload, mark)


def coefficients(ratios, pairs):
    signs = [1.0, 1.0, -1.0, -1.0]
    out = []
    for row in range(4):
        margin = jnp.zeros_like(ratios[0])
        for other in range(4):
            margin += jnp.where(pairs[other] == pairs[row], signs[other] * ratios[other], 0.0)
        out.append(-DPO_BETA * signs[row] / (1.0 + jnp.exp(DPO_BETA * margin)))
    return out


def coef_kernel(place, pairs, gathered, out, notes, sem):
    copy = pltpu.make_async_copy(
        gathered.at[:, pl.ds(gathered.shape[1] - EXTRA, EXTRA), pl.ds(0, 128)], notes, sem
    )
    copy.start()
    copy.wait()
    row = place[2]
    values = jnp.sum(notes[...].astype(F32).reshape(4, -1, EXTRA, notes.shape[2]), axis=1)

    def ratios(first):
        picked = values[:, :1, first : first + 3]
        return [jnp.sum(picked[r], axis=1, keepdims=True) for r in range(4)]

    first = notes[0, :1, :16].astype(F32)
    own = coefficients(ratios(OWN), [pairs[i].astype(F32) for i in range(4)])
    following = coefficients(ratios(0), [first[:, 3 + i : 4 + i] for i in range(4)])
    lane = lax.broadcasted_iota(jnp.int32, out.shape, 1)
    result = jnp.zeros(out.shape, F32)
    for r in range(4):
        result = jnp.where(lane == lax.rem(row - r + 4, 4), own[r], result)
        result = jnp.where((lane == 4) & (row == r), following[r], result)
    out[...] = result


def coef_table(place, pairs, gathered):
    scalar = pl.BlockSpec(memory_space=pltpu.SMEM)
    return pl.pallas_call(
        coef_kernel,
        in_specs=[scalar, scalar, ANYWHERE],
        out_specs=pl.BlockSpec(memory_space=pltpu.VMEM),
        out_shape=jax.ShapeDtypeStruct((8, 128), F32),
        scratch_shapes=[
            pltpu.VMEM((gathered.shape[0], EXTRA, 128), BF),
            pltpu.SemaphoreType.DMA,
        ],
        cost_estimate=FREE,
    )(place, pairs, gathered)


def finish_kernel(coefs, first, second, third, fourth, gains, weights, out, sums):
    total = first[...] * coefs[:1, :1]
    for i, wave in enumerate((second, third, fourth)):
        total += wave[...].astype(F32) * coefs[:1, i + 1 : i + 2]
    out[...] = (total * as_column(gains[...])).astype(BF)
    found = jnp.sum(total * weights[...].astype(F32), axis=1, keepdims=True)
    sums[...] = jnp.broadcast_to(found, (found.shape[0], 128)).T[:1].astype(BF)


def finished(coefs, waves, gains, weights):
    whole = pl.BlockSpec(memory_space=pltpu.VMEM)
    rows, kw = weights.shape
    return pl.pallas_call(
        finish_kernel,
        in_specs=[whole] * 7,
        out_specs=[whole] * 2,
        out_shape=[jax.ShapeDtypeStruct((rows, kw), BF), jax.ShapeDtypeStruct((1, rows), BF)],
        cost_estimate=FREE,
    )(coefs, *waves, gains, weights)


ORDER = (2, 1, 3, 0)


def block_products(spot, other, hidden, keys, terms, out, sem):
    y, z = spot[1], spot[2]
    core = 1 - spot[0] if other else spot[0]
    for r in ORDER:

        def block(q, carry):
            at = lax.rem(z + q, 4) * 8 + lax.rem(y + r, 4) * 2 + core
            columns = hidden[:, pl.ds(pl.multiple_of(at * BLK, BLK), BLK)]
            terms[r, q] = lax.dot_general(
                columns, keys[...], (((0,), (0,)), ((), ())), preferred_element_type=F32
            ).astype(BF)
            return carry

        lax.fori_loop(0, 4, block, 0)
        pltpu.make_async_copy(terms.at[r], out.at[r], sem.at[r]).start()
    for r in ORDER:
        pltpu.make_async_copy(terms.at[r], out.at[r], sem.at[r]).wait()


def load(source, target, sem, parts):
    rows = source.shape[0] // parts
    copies = []
    for i in range(parts):
        at = pl.ds(i * rows, rows)
        copies.append(pltpu.make_async_copy(source.at[at], target.at[at], sem.at[i]))
        copies[-1].start()
    return copies


def send_kernel(spot, payload, hidden, *refs):
    out, *quarters, keys, states, terms, in_sem, out_sem, row_sem = refs
    parts = 4
    rows = states.shape[0] // parts
    for i, copy in enumerate(load(hidden, states, in_sem, parts)):
        copy.wait()

        def line(j, carry):
            at = pl.ds(pl.multiple_of(i * rows + j * 16, 16), 16)
            square = jnp.zeros((16, 512), F32)
            for c in range(0, states.shape[1], 512):
                part = states[at, c : c + 512].astype(F32)
                square = square + part * part
            inv = lax.rsqrt(jnp.sum(square, axis=1, keepdims=True) / states.shape[1] + EPS)
            from_key = pl.ds(pl.multiple_of(states.shape[0] + EXTRA + i * rows + j * 16, 16), 16)
            keys[at, :] = (payload[from_key, :].astype(F32) * inv).astype(BF)
            return carry

        lax.fori_loop(0, rows // 16, line, 0)
    copies = [
        pltpu.make_async_copy(states.at[pl.ds(i * QUARTER, QUARTER)], quarter, row_sem.at[i])
        for i, quarter in enumerate(quarters)
    ]
    for copy in copies:
        copy.start()
    block_products(spot, True, states, keys, terms, out, out_sem)
    for copy in copies:
        copy.wait()


def keep_kernel(spot, keys, hidden, *refs):
    out, states, terms, in_sem, out_sem, _ = refs
    for copy in load(hidden, states, in_sem, 4):
        copy.wait()
    block_products(spot, False, states, keys, terms, out, out_sem)


def term_call(kernel, operands, sending):
    tokens, width = operands[2].shape
    kw = operands[1].shape[1]
    whole = pl.BlockSpec(memory_space=pltpu.VMEM)
    more = [jax.ShapeDtypeStruct((QUARTER, width), BF)] * 4 if sending else []
    keys = [jax.ShapeDtypeStruct((tokens, kw), BF)] if sending else []
    return pl.pallas_call(
        kernel,
        in_specs=[pl.BlockSpec(memory_space=pltpu.SMEM), whole, ANYWHERE],
        out_specs=[ANYWHERE] * (1 + len(more)) + [whole] * len(keys),
        out_shape=[jax.ShapeDtypeStruct((4, 4, BLK, kw), BF), *more, *keys],
        scratch_shapes=[
            pltpu.VMEM((tokens, width), BF),
            pltpu.VMEM((4, 4, BLK, kw), BF),
            pltpu.SemaphoreType.DMA((4,)),
            pltpu.SemaphoreType.DMA((4,)),
            pltpu.SemaphoreType.DMA((4,)),
        ],
        compiler_params=pltpu.CompilerParams(vmem_limit_bytes=VMEM_LIMIT),
        cost_estimate=FREE,
    )(*operands)


def around(value, steps):
    return moved(value, lambda z_hi, x, z_lo, y, core: (z_hi, x, z_lo, (y + steps) % 4, core))


def along(value, steps):
    return moved(value, lambda z_hi, x, z_lo, y, core: (z_hi, x, (z_lo + steps) % 4, y, core))


def added(*parts):
    return sum(part.astype(F32) for part in parts)


def grad_kernel(payload, weights, out, held, slopes, in_sem, out_sem):
    tokens, parts = out.shape[0], in_sem.shape[0]
    count, rows, kw = held.shape
    step = count // parts
    keys = payload[payload.shape[0] - tokens :, :]
    copies = []
    for i in range(parts):
        at = pl.ds(i * step, step)
        copies.append(
            pltpu.make_async_copy(weights.at[at, pl.ds(0, rows)], held.at[at], in_sem.at[i])
        )
        copies[-1].start()
    for i in range(parts):
        copies[i].wait()
        block = held[i * step : (i + 1) * step].reshape(step * rows, kw)
        span = pl.ds(i * step * rows, step * rows)
        slopes[:, span] = lax.dot_general(
            keys, block, (((1,), (1,)), ((), ())), preferred_element_type=F32
        ).astype(BF)
        copies[i] = pltpu.make_async_copy(slopes.at[:, span], out.at[:, span], out_sem.at[i])
        copies[i].start()
    for copy in copies:
        copy.wait()


def unit_grads(payload, gathered, tokens):
    count, _, kw = gathered.shape
    parts = 4
    return pl.pallas_call(
        grad_kernel,
        in_specs=[pl.BlockSpec(memory_space=pltpu.VMEM), ANYWHERE],
        out_specs=ANYWHERE,
        out_shape=jax.ShapeDtypeStruct((tokens, count * BLK), BF),
        scratch_shapes=[
            pltpu.VMEM((count, BLK, kw), BF),
            pltpu.VMEM((tokens, count * BLK), BF),
            pltpu.SemaphoreType.DMA((parts,)),
            pltpu.SemaphoreType.DMA((parts,)),
        ],
        compiler_params=pltpu.CompilerParams(vmem_limit_bytes=VMEM_LIMIT),
        cost_estimate=FREE,
    )(payload, gathered)


def section_kernel(near_rows, far_rows, scale, is_far, slopes, *refs):
    count = len(near_rows)
    near, far = refs[:count], refs[count : count + len(far_rows)]
    out, rows, grads, done, row_sem, grad_sem, out_sem = refs[count + len(far_rows) :]
    tokens, width = rows.shape
    group, span = 16, 512
    parts = tokens // PIECE

    def fetched(sources, sizes):
        first = 0
        for source, size in zip(sources, sizes):
            for at in range(0, size, PIECE):
                spot = (first + at) // PIECE
                pltpu.make_async_copy(
                    source.at[pl.ds(at, PIECE)], rows.at[pl.ds(first + at, PIECE)], row_sem.at[spot]
                ).start()
            first += size

    def whole(i):
        return pl.ds(pl.multiple_of(i * PIECE, PIECE), PIECE)

    for i in range(parts):
        at = pl.ds(i * PIECE, PIECE)
        pltpu.make_async_copy(slopes.at[at], grads.at[at], grad_sem.at[i]).start()

    @pl.when(is_far[0] == 1)
    def _():
        fetched(far, far_rows)

    @pl.when(is_far[0] != 1)
    def _():
        fetched(near, near_rows)

    factor = scale[:1, 4:5]

    def part(i, carry):
        at = whole(i)
        pltpu.make_async_copy(slopes.at[at], grads.at[at], grad_sem.at[i]).wait()
        pltpu.make_async_copy(slopes.at[at], rows.at[at], row_sem.at[i]).wait()
        for g in range(PIECE // group):
            line = pl.ds(pl.multiple_of(i * PIECE + g * group, group), group)
            square = jnp.zeros((group, span), F32)
            cross = jnp.zeros((group, span), F32)
            for c in range(0, width, span):
                h = rows[line, c : c + span].astype(F32)
                square = square + h * h
                cross = cross + h * grads[line, c : c + span].astype(F32)
            inv = lax.rsqrt(jnp.sum(square, axis=1, keepdims=True) / width + EPS)
            inner = jnp.sum(cross, axis=1, keepdims=True) / width * inv * factor
            ahead, back = inv * factor, inv * inv * inner
            for c in range(0, width, span):
                h = rows[line, c : c + span].astype(F32)
                u = grads[line, c : c + span].astype(F32)
                done[line, c : c + span] = (ahead * u - back * h).astype(BF)
        pltpu.make_async_copy(done.at[at], out.at[at], out_sem.at[i]).start()
        return carry

    lax.fori_loop(0, parts, part, 0)
    for i in range(parts):
        at = pl.ds(i * PIECE, PIECE)
        pltpu.make_async_copy(done.at[at], out.at[at], out_sem.at[i]).wait()


def section_grads(scale, is_far, slopes, near, far):
    tokens, width = slopes.shape
    scalar = pl.BlockSpec(memory_space=pltpu.SMEM)
    near_rows, far_rows = [v.shape[0] for v in near], [v.shape[0] for v in far]
    parts = tokens // PIECE
    return pl.pallas_call(
        functools.partial(section_kernel, near_rows, far_rows),
        in_specs=[pl.BlockSpec(memory_space=pltpu.VMEM), scalar] + [ANYWHERE] * (1 + len(near) + len(far)),
        out_specs=ANYWHERE,
        out_shape=jax.ShapeDtypeStruct((tokens, width), BF),
        scratch_shapes=[pltpu.VMEM((tokens, width), BF)] * 3
        + [pltpu.SemaphoreType.DMA((parts,))] * 3,
        compiler_params=pltpu.CompilerParams(vmem_limit_bytes=VMEM_LIMIT),
        cost_estimate=FREE,
    )(scale, is_far, slopes, *near, *far)


def on_device(hidden, norm_gain, key_weight, key_cotangent, token_logratio, lengths, pair_of_row):
    states = hidden[0]
    weights = key_weight[0]
    tokens, width = states.shape
    kw = weights.shape[1]
    section, dp = lax.axis_index("section"), lax.axis_index("dp")
    core, y, z = dp % 2, (dp // 2) % 4, dp // 8
    place = jnp.stack([core, y, z, (dp * tokens) % ROW_LEN]).astype(jnp.int32)

    payload, mark = prepared(
        place, lengths[0], pair_of_row[0], weights, norm_gain, key_cotangent[0], token_logratio
    )
    following = to_previous(payload)

    send, *quarters, keys = term_call(send_kernel, (place, payload, states), True)
    following = gated([following], [keys])[0]
    joint = joined(following, mark)
    send = gated([send], [joint])[0]
    gathered = lax.all_gather(joint, "dp", axis=0, tiled=True)
    gathered = gathered.reshape(-1, tokens + EXTRA, kw)
    near = lowered(states)
    up = (1, 0)
    direct = stepped(quarters[0], up, (0, 3))
    spread = {x: stepped(quarters[x], up, (1, x)) for x in (2, 3, 1)}

    def over_cores(operands):
        states, keys, place, send = operands
        swapped = moved(send, lambda z_hi, x, z_lo, y, core: (z_hi, x, z_lo, y, 1 - core))
        return swapped, *term_call(keep_kernel, (place, keys, states), False)

    def over_far_chips(operands):
        swapped, keep = operands
        sums = lambda r, *more: added(keep[r], swapped[r], *more)
        far = sums(2).astype(BF)
        far_up, far_down = around(far[:2], 1), around(far[2:], -1)
        up_terms = jnp.concatenate([far_up.astype(F32), jnp.zeros(far_up.shape, F32)])
        down_terms = jnp.concatenate([jnp.zeros(far_down.shape, F32), far_down.astype(F32)])
        return sums(0).astype(BF), sums(1, up_terms).astype(BF), sums(3, down_terms).astype(BF)

    def over_chips(operands):
        here, up_terms, down_terms = operands
        plane = added(here, around(up_terms, 1), around(down_terms, -1))
        return plane[0], *[plane[i].astype(BF) for i in (1, 2, 3)]

    def staged(step, operands):
        shapes = jax.eval_shape(step, operands)
        blank = lambda _: jax.tree.map(lambda v: jnp.zeros(v.shape, v.dtype), shapes)
        return lax.cond(dp < tokens, step, blank, operands)

    sums = staged(over_cores, (states, keys, place, send))
    second, third, first = gated([spread[x] for x in (2, 3, 1)], sums[:1])
    crossing = picked(section, [first, second, third])
    crossed = moved(
        crossing, lambda z_hi, x, z_lo, y, core: (0, x, z_lo, y, core) if z_hi and x else None
    )
    plane = staged(over_chips, staged(over_far_chips, sums))
    crossed = gated([crossed], plane[:1])[0]
    far = [direct, *[stepped(crossed, (0, x), (0, 3)) for x in (1, 2)], crossed]
    slopes = unit_grads(following, gathered, tokens)
    coefs = coef_table(place, pair_of_row[0], gathered)
    later = gated(plane[1:], [near])
    slopes = gated([slopes], [coefs])[0]
    first, last = along(later[0], 1), along(later[2], 3)
    middle = along(gated([later[1]], [slopes])[0], 2)
    waves = [plane[0], first, middle, last]

    is_far = (section == 3).astype(jnp.int32)[None]
    out = section_grads(coefs, is_far, slopes, [near], far)
    waves[2] = gated([waves[2]], [out])[0]
    weight_grad, gain_grad = finished(coefs, waves, norm_gain, weights)
    return out[None], weight_grad[None], gain_grad


def solution(mesh):
    in_specs = (
        P("section", "dp", None),
        P("section", "dp"),
        P("section", "dp", None),
        P("section", "dp", None),
        P("section", "dp"),
        P("section", None),
        P("section", None),
    )
    out_specs = (P("section", "dp", None), P("section", "dp", None), P("section", "dp"))
    return jax.shard_map(
        on_device, mesh=mesh, in_specs=in_specs, out_specs=out_specs, check_vma=False
    )
```
